128 devices in a mesh: sec: 4 (over x), fsdp: 4 (over y_hi, core), tp: 8 (over y_lo, z).
Axes of the slice: x: 4, y: 4 (y_hi: 2, y_lo: 2; y = y_hi * 2 + y_lo), z: 4, core: 2. Of those that a mesh axis runs over, the one named last changes fastest.
Arguments:
- layer_input: bfloat16 [65536, 5120], P(('sec', 'fsdp'), 'tp'), may hold values from -6 to 6
- value_cotangent: bfloat16 [65536, 1024], P(('sec', 'fsdp')), may hold values from -6 to 6
- value_weight: bfloat16 [1024, 5120], P(('sec', 'fsdp'), 'tp'), may hold values from -0.078125 to 0.078125
- rewards: float32 [64], replicated, may hold values from -3 to 3
- group_ids: int32 [64], replicated, may hold values from 0 to 7, as said below
- prompt_lengths: int32 [64], replicated, may hold values from 128 to 895
- step_inputs: bfloat16 [4, 64, 5120], P(None, ('sec', 'fsdp')), may hold values from -6 to 6
- queries: bfloat16 [4, 64, 8192], P(None, ('sec', 'fsdp'), 'tp'), may hold values from -24 to 24
- key_weight: bfloat16 [1024, 5120], P('tp'), may hold values from -0.078125 to 0.078125
- cache_keys: bfloat16 [64, 2048, 1024], P(('sec', 'fsdp'), None, 'tp'), may hold values from -6 to 6
- cache_values: bfloat16 [64, 2048, 1024], P(('sec', 'fsdp'), None, 'tp'), may hold values from -6 to 6
- cache_lengths: int32 [64], P(('sec', 'fsdp')), may hold values from 256 to 2048
Outputs:
- input_grad: bfloat16 [65536, 5120], P(('sec', 'fsdp'), 'tp')
- new_keys: bfloat16 [4, 64, 1024], P(None, ('sec', 'fsdp'), 'tp')
- new_values: bfloat16 [4, 64, 1024], P(None, ('sec', 'fsdp'), 'tp')
- attended: bfloat16 [4, 64, 8192], P(None, ('sec', 'fsdp'), 'tp')
The draws below stay inside these ranges and needn't reach their ends.
Inputs may be any that keep to these rules, and one draw needn't show every extreme that they name: `group_ids`: each group id names exactly 8 sequences.
All inputs are finite; a program needn't handle non-finite values.
Results may differ from the reference program's by a relative error of at most 0.0052.
Values may be sent and summed in bfloat16 or wider, within the bound.
A program may use at most 128 MiB of HBM per device.

```python
import jax
import jax.numpy as jnp
from jax import lax

D = 5120
KV_HEADS = 8
HEAD = 128
QPK = 8
KVW = 1024
QW = 8192
SEQ_LEN = 1024
GROUP = 8
TOKENS = 65536
SEQS = 64
ROWS = 64
CACHE = 2048
STEPS = 4


def draw_queries(key, part):
    key = jax.random.fold_in(key, 1)
    values = jnp.clip(jax.random.normal(key, (STEPS, ROWS, QW), jnp.float32), -6.0, 6.0)
    return values.astype(jnp.bfloat16)


def draw_cache_keys(key, part):
    key = jax.random.fold_in(key, 2)
    base_key = jax.random.fold_in(key, 0)
    values = jnp.clip(jax.random.normal(base_key, (ROWS, CACHE, KVW), jnp.float32), -6.0, 6.0)
    return values.astype(jnp.bfloat16)


def draw_cache_lengths(key, part):
    key = jax.random.fold_in(key, 3)
    lengths = jax.random.randint(key, (ROWS,), CACHE // 8, CACHE + 1)
    lengths = lengths.at[0].set(CACHE)
    lengths = lengths.at[1].set(CACHE // 8)
    return lengths.astype(jnp.int32)


def draw_prompt_lengths(key, part):
    key = jax.random.fold_in(key, 4)
    index = jnp.arange(SEQS, dtype=jnp.int32)
    ramp = SEQ_LEN * 5 // 8 * (SEQS - 1 - index) // max(SEQS - 1, 1)
    jitter = jax.random.randint(key, (SEQS,), 0, SEQ_LEN // 8)
    lengths = SEQ_LEN // 8 + ramp + jitter
    lengths = lengths.at[0].set(SEQ_LEN * 7 // 8 - 1)
    lengths = lengths.at[SEQS - 1].set(SEQ_LEN // 8)
    return lengths.astype(jnp.int32)


def draw_group_ids(key, part):
    key = jax.random.fold_in(key, 5)
    order = jax.random.permutation(key, SEQS)
    return (order // GROUP).astype(jnp.int32)


def level_of(own_key, dims, pieces, least, top_value):
    gain = 1.0
    for axis_at, blocks in pieces:
        draws = jax.random.uniform(jax.random.fold_in(jax.random.fold_in(own_key, 6), axis_at), (blocks,), jnp.float32, least / len(pieces), top_value / len(pieces))
        gain = gain * jnp.repeat(jnp.exp(draws), dims[axis_at] // blocks).reshape((-1,) + (1,) * (len(dims) - 1 - axis_at))
    return gain


def gaussian(key, shape, deviation, bound, shards=(), kind=jnp.bfloat16):
    factor_of = level_of(key, shape, shards, -0.22, 0.18) if shards else 1.0
    entries = jax.random.normal(key, shape, jnp.float32) * deviation * factor_of
    return jnp.minimum(jnp.maximum(entries, -bound), bound).astype(kind)


def setup_inputs(seed: int = 0) -> dict:
    splits = jax.random.split(jax.random.key(seed), 13)
    return {
        "layer_input": gaussian(splits[0], (TOKENS, D), 1.0, 6.0, ((0, 16), (1, 8))),
        "value_cotangent": gaussian(splits[1], (TOKENS, KVW), 1.0, 6.0, ((0, 16),)),
        "value_weight": gaussian(splits[2], (KVW, D), D ** -0.5, 0.078125, ((0, 16), (1, 8))),
        "rewards": jnp.clip(jax.random.uniform(splits[3], (SEQS,), jnp.float32, -3.0, 3.0), -3.0, 3.0),
        "group_ids": draw_group_ids(jax.random.fold_in(splits[12], 71), 0),
        "prompt_lengths": draw_prompt_lengths(jax.random.fold_in(splits[12], 71), 0),
        "step_inputs": gaussian(splits[6], (STEPS, ROWS, D), 1.0, 6.0, ((1, 16),)),
        "queries": draw_queries(jax.random.fold_in(splits[12], 71), 0),
        "key_weight": gaussian(splits[8], (KVW, D), D ** -0.5, 0.078125, ((0, 8),)),
        "cache_keys": draw_cache_keys(jax.random.fold_in(splits[12], 71), 0),
        "cache_values": gaussian(splits[10], (ROWS, CACHE, KVW), 1.0, 6.0, ((0, 16), (2, 8))),
        "cache_lengths": draw_cache_lengths(jax.random.fold_in(splits[12], 71), 0),
    }


def reference(layer_input, value_cotangent, value_weight, rewards, group_ids, prompt_lengths, step_inputs, queries, key_weight, cache_keys, cache_values, cache_lengths):
    same = (group_ids[:, None] == group_ids[None, :]).astype(jnp.float32)
    advantage = rewards - jnp.sum(same * rewards[None, :], axis=1) / GROUP
    positions = jnp.arange(TOKENS, dtype=jnp.int32)
    seq_index = positions // SEQ_LEN
    offsets = positions % SEQ_LEN
    response = offsets >= prompt_lengths[seq_index]
    token_weight = jnp.where(response, advantage[seq_index], jnp.float32(0.0))
    weighted = (value_cotangent.astype(jnp.float32) * token_weight[:, None]).astype(jnp.bfloat16)
    responses = jnp.sum(response.astype(jnp.float32))
    weight_sum = lax.dot_general(weighted, layer_input, (((0,), (0,)), ((), ())), preferred_element_type=jnp.float32)
    new_weight = value_weight.astype(jnp.float32) - weight_sum / responses
    input_grad = jnp.dot(weighted, value_weight, preferred_element_type=jnp.float32).astype(jnp.bfloat16)
    flat = step_inputs.reshape(STEPS * ROWS, D)
    contract = (((1,), (1,)), ((), ()))
    new_keys = lax.dot_general(flat, key_weight, contract, preferred_element_type=jnp.float32).astype(jnp.bfloat16).reshape(STEPS, ROWS, KVW)
    new_values = lax.dot_general(flat.astype(jnp.float32), new_weight, contract, precision=lax.Precision.HIGHEST, preferred_element_type=jnp.float32).astype(jnp.bfloat16).reshape(STEPS, ROWS, KVW)
    scale = 1.0 / (HEAD ** 0.5)

    def one_row(item):
        query, ckeys, cvals, length, fkeys, fvals = item
        query4 = query.astype(jnp.float32).reshape(STEPS, KV_HEADS, QPK, HEAD)
        ck3 = ckeys.astype(jnp.float32).reshape(CACHE, KV_HEADS, HEAD)
        cv3 = cvals.astype(jnp.float32).reshape(CACHE, KV_HEADS, HEAD)
        fk3 = fkeys.astype(jnp.float32).reshape(STEPS, KV_HEADS, HEAD)
        fv3 = fvals.astype(jnp.float32).reshape(STEPS, KV_HEADS, HEAD)
        cache_scores = jnp.einsum('skqd,ckd->skqc', query4, ck3) * scale
        fresh_scores = jnp.einsum('skqd,tkd->skqt', query4, fk3) * scale
        live = (jnp.arange(CACHE, dtype=jnp.int32) < length)[None, None, None, :]
        steps_idx = jnp.arange(STEPS, dtype=jnp.int32)
        causal = (steps_idx[None, :] <= steps_idx[:, None])[:, None, None, :]
        cache_scores = jnp.where(live, cache_scores, jnp.float32(-1e30))
        fresh_scores = jnp.where(causal, fresh_scores, jnp.float32(-1e30))
        top = jnp.maximum(jnp.max(cache_scores, axis=-1, keepdims=True), jnp.max(fresh_scores, axis=-1, keepdims=True))
        cache_exp = jnp.where(live, jnp.exp(cache_scores - top), jnp.float32(0.0))
        fresh_exp = jnp.where(causal, jnp.exp(fresh_scores - top), jnp.float32(0.0))
        total = jnp.sum(cache_exp, axis=-1, keepdims=True) + jnp.sum(fresh_exp, axis=-1, keepdims=True)
        cache_prob = (cache_exp / total).astype(jnp.bfloat16).astype(jnp.float32)
        fresh_prob = (fresh_exp / total).astype(jnp.bfloat16).astype(jnp.float32)
        output = jnp.einsum('skqc,ckd->skqd', cache_prob, cv3) + jnp.einsum('skqt,tkd->skqd', fresh_prob, fv3)
        return output.astype(jnp.bfloat16).reshape(STEPS, QW)

    attended = lax.map(one_row, (jnp.transpose(queries, (1, 0, 2)), cache_keys, cache_values, cache_lengths, jnp.transpose(new_keys, (1, 0, 2)), jnp.transpose(new_values, (1, 0, 2))))
    attended = jnp.transpose(attended, (1, 0, 2))
    return input_grad, new_keys, new_values, attended
```

```python
import functools

import jax
import jax.numpy as jnp
from jax import lax
from jax.experimental import pallas as pl
from jax.experimental.pallas import tpu as pltpu
from jax.sharding import PartitionSpec as P

HEAD = 128
QPK = 8
SEQ_LEN = 1024
GROUP = 8
SKIP = 128
LIVE = SEQ_LEN - SKIP
MESH = pl.DeviceIdType.MESH
F32 = jnp.float32
BF16 = jnp.bfloat16
NT = (((1,), (1,)), ((), ()))
NN = (((1,), (0,)), ((), ()))


def flip(value, bits):
    for at in range(3):
        unit = 1 << at
        if bits & unit:
            value = value + unit - 2 * unit * lax.rem(lax.div(value, unit), 2)
    return value


def dot(a, b, dims):
    return lax.dot_general(a, b, dims, preferred_element_type=F32)


def kernel(
    layer_ref,
    cot_ref,
    vw_ref,
    rewards_ref,
    groups_ref,
    prompts_ref,
    step_ref,
    query_ref,
    kw_ref,
    ck_ref,
    cv_ref,
    len_ref,
    grad_ref,
    nk_ref,
    nv_ref,
    att_ref,
    layer_v,
    cot_v,
    vw_v,
    step_v,
    query_v,
    kw_v,
    ck_v,
    cv_v,
    flat_v,
    xall_v,
    wall_v,
    a_v,
    away_v,
    home_v,
    core_v,
    recv_v,
    out_v,
    zero_v,
    att_v,
    load_sem,
    out_sem,
    zero_sem,
    x_send,
    x_recv,
    w_send,
    w_recv,
    pair_send,
    pair_recv,
    core_send,
    core_recv,
    rs_send,
    rs_recv,
    ready_sem,
):
    sec = lax.axis_index("sec")
    fs = lax.axis_index("fsdp")
    tp = lax.axis_index("tp")
    core = lax.rem(fs, 2)
    group = sec * 4 + fs
    seqs = layer_ref.shape[0] // SEQ_LEN
    n_seq = rewards_ref.shape[0]
    cols = layer_ref.shape[1]

    def device(q, dc, dt):
        return (flip(sec, q // 2), flip(fs, (q % 2) * 2 + dc), flip(tp, dt))

    barrier = pltpu.get_barrier_semaphore()
    for q in range(8):
        for dc in range(2):
            if q or dc:
                pl.semaphore_signal(barrier, inc=1, device_id=device(q, dc, 0), device_id_type=MESH)
    for dt in range(1, 8):
        pl.semaphore_signal(barrier, inc=1, device_id=device(0, 0, dt), device_id_type=MESH)

    def load(src, dst, at):
        copy = pltpu.make_async_copy(src, dst, load_sem.at[at])
        copy.start()
        return copy

    step_load = load(step_ref, step_v, 0)
    vw_load = load(vw_ref, vw_v, 1)
    query_load = load(query_ref, query_v, 2)
    kw_load = load(kw_ref, kw_v, 3)
    rows_n = ck_ref.shape[0]
    ck_loads = [load(ck_ref.at[r], ck_v.at[r], 4 + r) for r in range(rows_n)]
    cv_loads = [load(cv_ref.at[r], cv_v.at[r], 8 + r) for r in range(rows_n)]
    cot_loads = [
        load(cot_ref.at[pl.ds(s * SEQ_LEN + SKIP, LIVE)], cot_v.at[pl.ds(s * LIVE, LIVE)], 12 + s)
        for s in range(seqs)
    ]
    layer_loads = [
        load(layer_ref.at[pl.ds(s * SEQ_LEN + SKIP, LIVE)], layer_v.at[pl.ds(s * LIVE, LIVE)], 16 + s)
        for s in range(seqs)
    ]

    zero_v[...] = jnp.zeros_like(zero_v)
    zero_copies = [
        pltpu.make_async_copy(zero_v, grad_ref.at[pl.ds(s * SEQ_LEN, SKIP)], zero_sem.at[s])
        for s in range(seqs)
    ]
    for copy in zero_copies:
        copy.start()

    first = group * seqs
    own_groups = [groups_ref[first + s] for s in range(seqs)]
    own_prompts = [prompts_ref[first + s] for s in range(seqs)]

    def scan(j, carry):
        prompts = carry[0] + prompts_ref[j]
        reward = rewards_ref[j]
        sums = [
            c + jnp.where(groups_ref[j] == g, reward, F32(0.0))
            for c, g in zip(carry[1:], own_groups)
        ]
        return (prompts, *sums)

    scanned = lax.fori_loop(0, n_seq, scan, (jnp.int32(0),) + (F32(0.0),) * seqs)
    responses = (n_seq * SEQ_LEN - scanned[0]).astype(F32)
    advantage = [rewards_ref[first + s] - scanned[1 + s] / F32(GROUP) for s in range(seqs)]

    step_load.wait()
    flat_v[...] = jnp.concatenate(
        [step_v[s].astype(F32) for s in range(step_v.shape[0])], axis=0
    ).astype(BF16)
    own_x = flat_v.at[:, pl.ds(pl.multiple_of(tp * cols, 128), cols)]
    xall_v[0] = flat_v[:, pl.ds(pl.multiple_of(tp * cols, 128), cols)]
    vw_load.wait()
    wall_v[sec * 2 + lax.div(fs, 2), core] = vw_v[...]

    pl.semaphore_wait(barrier, 22)
    for dt in range(1, 8):
        pl.semaphore_signal(ready_sem, inc=1, device_id=device(0, 0, dt), device_id_type=MESH)
    for dc in (0, 1):
        for q in range(8):
            if q or dc:
                pltpu.make_async_remote_copy(
                    src_ref=own_x,
                    dst_ref=xall_v.at[dc * 8 + q],
                    send_sem=x_send,
                    recv_sem=x_recv,
                    device_id=device(q, dc, 0),
                    device_id_type=MESH,
                ).start()
    for q in range(1, 8):
        pltpu.make_async_remote_copy(
            src_ref=vw_v,
            dst_ref=wall_v.at[sec * 2 + lax.div(fs, 2), core],
            send_sem=w_send,
            recv_sem=w_recv,
            device_id=device(q, 0, 0),
            device_id_type=MESH,
        ).start()

    kw_load.wait()
    new_keys = dot(flat_v[...], kw_v[...], NT).astype(BF16)
    nk_ref[...] = new_keys

    query_load.wait()
    steps_n = query_v.shape[0]
    q16 = jnp.concatenate([query_v[s].astype(F32) for s in range(steps_n)], axis=0).astype(BF16)
    stacked = jnp.concatenate([q16[:, h * HEAD : (h + 1) * HEAD] for h in range(QPK)], axis=0)
    n_q = QPK * steps_n * rows_n
    to_r = lax.broadcasted_iota(jnp.int32, (n_q, n_q), 0)
    frm = lax.broadcasted_iota(jnp.int32, (n_q, n_q), 1)
    per = steps_n * QPK
    src_of = lax.rem(to_r, QPK) * 16 + lax.rem(lax.div(to_r, QPK), steps_n) * rows_n + lax.div(to_r, per)
    perm = (frm == src_of).astype(F32).astype(BF16)
    scale = F32(1.0 / HEAD**0.5)
    queries = dot(perm, stacked, NN).astype(BF16)
    fresh = dot(queries, new_keys, NT) * scale
    i_at = lax.broadcasted_iota(jnp.int32, fresh.shape, 0)
    j_at = lax.broadcasted_iota(jnp.int32, fresh.shape, 1)
    causal = (lax.div(i_at, per) == lax.rem(j_at, rows_n)) & (
        lax.div(j_at, rows_n) <= lax.rem(lax.div(i_at, QPK), steps_n)
    )
    fresh = jnp.where(causal, fresh, F32(-1e30))
    fresh_top = jnp.max(fresh, axis=1, keepdims=True)
    slots = ck_v.shape[1]
    slot_at = lax.broadcasted_iota(jnp.int32, (per, slots), 1)
    fresh_probs = []
    for r in range(rows_n):
        part = slice(r * per, (r + 1) * per)
        ck_loads[r].wait()
        scores = dot(queries[part], ck_v[r], NT) * scale
        live = slot_at < len_ref[r]
        scores = jnp.where(live, scores, F32(-1e30))
        top = jnp.maximum(jnp.max(scores, axis=1, keepdims=True), fresh_top[part])
        e = jnp.where(live, jnp.exp(scores - top), F32(0.0))
        fe = jnp.where(causal[part], jnp.exp(fresh[part] - top), F32(0.0))
        total = jnp.sum(e, axis=1, keepdims=True) + jnp.sum(fe, axis=1, keepdims=True)
        inv = F32(1.0) / total
        cv_loads[r].wait()
        att_v[part, :] = dot((e * inv).astype(BF16), cv_v[r], NN)
        fresh_probs.append((fe * inv).astype(BF16).astype(F32))
    fresh_prob = jnp.concatenate(fresh_probs, axis=0).astype(BF16)

    rows_at = lax.broadcasted_iota(jnp.int32, (128, 128), 0)
    wide = cot_v.shape[1]
    for s in range(seqs):
        cot_loads[s].wait()

        def weigh(j, _, s=s):
            at = pl.multiple_of(s * LIVE + j * 128, 128)
            weight = jnp.where(rows_at + (SKIP + j * 128) >= own_prompts[s], advantage[s], F32(0.0))
            for n in range(wide // 128):
                span = slice(n * 128, (n + 1) * 128)
                cot_v[pl.ds(at, 128), span] = (cot_v[pl.ds(at, 128), span].astype(F32) * weight).astype(BF16)
            return 0

        lax.fori_loop(0, LIVE // 128, weigh, 0)

    pltpu.make_async_copy(xall_v.at[pl.ds(1, 15)], xall_v.at[pl.ds(1, 15)], x_recv).wait()
    x_all = xall_v[...].reshape(256, cols)
    for copy in layer_loads:
        copy.wait()
    tokens = layer_v.shape[0]
    blk = 512

    def outer(j, _):
        at = pl.multiple_of(j * blk, blk)
        a_v[:, pl.ds(at, blk)] = dot(xall_v[...].reshape(256, cols), layer_v[pl.ds(at, blk), :], NT).astype(BF16)
        return 0

    lax.fori_loop(0, tokens // blk, outer, 0)

    pltpu.make_async_copy(wall_v.at[pl.ds(0, 7), 0], wall_v.at[pl.ds(0, 7), 0], w_recv).wait()
    pair = pltpu.make_async_remote_copy(
        src_ref=wall_v.at[:, core],
        dst_ref=wall_v.at[:, core],
        send_sem=pair_send,
        recv_sem=pair_recv,
        device_id=device(0, 1, 0),
        device_id_type=MESH,
    )
    pair.start()

    inv_resp = F32(1.0) / responses
    own = dot(x_all, jnp.concatenate([vw_v[...]] * 4, axis=0), NT)
    quarter = lax.div(lax.broadcasted_iota(jnp.int32, (256, 256), 1), 64)
    own = jnp.where(quarter == lax.rem(group, 4), own, F32(0.0))
    own_chunk = lax.div(group, 4)
    tp_hi, tp_lo = lax.div(tp, 2), lax.rem(tp, 2)
    copies = []
    for k in range(4):
        at = flip(tp_hi, k)
        weighted = cot_v[:, pl.ds(pl.multiple_of(at * 256, 256), 256)]
        part = jnp.where(own_chunk == at, own, F32(0.0)) - dot(a_v[...], weighted, NN) * inv_resp
        for j in range(2):
            home_v[k, j] = part[:128, j * 128 : (j + 1) * 128]
            away_v[k, j] = part[128:, j * 128 : (j + 1) * 128]
        copy = pltpu.make_async_remote_copy(
            src_ref=away_v.at[k],
            dst_ref=core_v.at[k],
            send_sem=core_send.at[k],
            recv_sem=core_recv.at[k],
            device_id=device(0, 1, 0),
            device_id_type=MESH,
        )
        copy.start()
        copies.append(copy)
    pl.semaphore_wait(ready_sem, 7)

    def scatter(k):
        copies[k].wait_recv()
        home_v[k] = home_v[k] + core_v[k]
        for e in range(2):
            j = flip(tp_lo, e)
            dt = 2 * k + e
            for q in range(8):
                if q or dt:
                    pltpu.make_async_remote_copy(
                        src_ref=home_v.at[k, j, pl.ds(q * 16, 16)],
                        dst_ref=recv_v.at[q * 8 + dt],
                        send_sem=rs_send,
                        recv_sem=rs_recv,
                        device_id=device(q, 0, dt),
                        device_id_type=MESH,
                    ).start()
        if k == 0:
            recv_v[0] = home_v[0, tp_lo, 0:16, :]

    for k in range(4):
        scatter(k)

    pair.wait()
    half = LIVE // 2

    def grad(j, _):
        at = pl.multiple_of(j * half, half)
        out_v[pl.ds(at, half), :] = dot(
            cot_v[pl.ds(at, half), :], wall_v[...].reshape(wide, cols), NN
        ).astype(BF16)
        to = lax.div(j, 2) * SEQ_LEN + SKIP + lax.rem(j, 2) * half
        pltpu.make_async_copy(
            out_v.at[pl.ds(at, half)], grad_ref.at[pl.ds(pl.multiple_of(to, 64), half)], out_sem
        ).start()
        return 0

    lax.fori_loop(0, tokens // half, grad, 0)

    pltpu.make_async_copy(recv_v.at[pl.ds(1, 63)], recv_v.at[pl.ds(1, 63)], rs_recv).wait()
    new_values = jnp.sum(recv_v[...], axis=0).astype(BF16)
    nv_ref[...] = new_values
    done = (att_v[...] + dot(fresh_prob, new_values, NN)).astype(BF16)
    back = dot(perm, done, (((0,), (0,)), ((), ()))).astype(BF16)
    for h in range(QPK):
        att_ref[:, h * HEAD : (h + 1) * HEAD] = back[h * 16 : (h + 1) * 16]

    pltpu.make_async_copy(recv_v.at[pl.ds(1, 63)], recv_v.at[pl.ds(1, 63)], rs_send).wait()
    pltpu.make_async_copy(xall_v.at[pl.ds(1, 15)], xall_v.at[pl.ds(1, 15)], x_send).wait()
    pltpu.make_async_copy(wall_v.at[pl.ds(0, 7), 0], wall_v.at[pl.ds(0, 7), 0], w_send).wait()
    for copy in copies:
        copy.wait_send()
    for copy in zero_copies:
        copy.wait()
    pltpu.make_async_copy(out_v, out_v, out_sem).wait()


def body(*args):
    layer, cot, vw, rewards, groups, prompts, step, query, kw, ck, cv, lengths = args
    steps_n, rows_n, width = step.shape
    n = steps_n * rows_n
    seqs = layer.shape[0] // SEQ_LEN
    tokens = seqs * LIVE
    cols = layer.shape[1]
    hbm = pl.BlockSpec(memory_space=pl.ANY)
    smem = pl.BlockSpec(memory_space=pltpu.SMEM)
    vmem = pl.BlockSpec(memory_space=pltpu.VMEM)
    dma = pltpu.SemaphoreType.DMA
    grad, new_keys, new_values, attended = pl.pallas_call(
        kernel,
        out_shape=(
            jax.ShapeDtypeStruct(layer.shape, BF16),
            jax.ShapeDtypeStruct((n, HEAD), BF16),
            jax.ShapeDtypeStruct((n, HEAD), BF16),
            jax.ShapeDtypeStruct((n, QPK * HEAD), BF16),
        ),
        in_specs=[hbm, hbm, hbm, smem, smem, smem, hbm, hbm, hbm, hbm, hbm, smem],
        out_specs=(hbm, vmem, vmem, vmem),
        scratch_shapes=[
            pltpu.VMEM((tokens, cols), BF16),
            pltpu.VMEM((tokens, cot.shape[1]), BF16),
            pltpu.VMEM(vw.shape, BF16),
            pltpu.VMEM(step.shape, BF16),
            pltpu.VMEM(query.shape, BF16),
            pltpu.VMEM(kw.shape, BF16),
            pltpu.VMEM(ck.shape, BF16),
            pltpu.VMEM(cv.shape, BF16),
            pltpu.VMEM((n, width), BF16),
            pltpu.VMEM((16, n, cols), BF16),
            pltpu.VMEM((8, 2, *vw.shape), BF16),
            pltpu.VMEM((256, tokens), BF16),
            pltpu.VMEM((4, 2, 128, 128), F32),
            pltpu.VMEM((4, 2, 128, 128), F32),
            pltpu.VMEM((4, 2, 128, 128), F32),
            pltpu.VMEM((64, n, HEAD), F32),
            pltpu.VMEM((tokens, cols), BF16),
            pltpu.VMEM((SKIP, cols), BF16),
            pltpu.VMEM((128, HEAD), F32),
            dma((20,)),
            dma,
            dma((4,)),
            dma,
            dma,
            dma,
            dma,
            dma,
            dma,
            dma((4,)),
            dma((4,)),
            dma,
            dma,
            pltpu.SemaphoreType.REGULAR,
        ],
        compiler_params=pltpu.CompilerParams(
            collective_id=0, has_side_effects=True, vmem_limit_bytes=56 * 1024 * 1024
        ),
    )(*args)
    return (
        grad,
        new_keys.reshape(steps_n, rows_n, HEAD),
        new_values.reshape(steps_n, rows_n, HEAD),
        attended.reshape(steps_n, rows_n, QPK * HEAD),
    )


def solution(mesh):
    tokens = ("sec", "fsdp")
    in_specs = (
        P(tokens, "tp"),
        P(tokens, None),
        P(tokens, "tp"),
        P(),
        P(),
        P(),
        P(None, tokens, None),
        P(None, tokens, "tp"),
        P("tp", None),
        P(tokens, None, "tp"),
        P(tokens, None, "tp"),
        P(tokens),
    )
    out_specs = (
        P(tokens, "tp"),
        P(None, tokens, "tp"),
        P(None, tokens, "tp"),
        P(None, tokens, "tp"),
    )
    return jax.shard_map(body, mesh=mesh, in_specs=in_specs, out_specs=out_specs, check_vma=False)
```

```python
import functools

import jax
import jax.numpy as jnp
from jax import lax
from jax.experimental import pallas as pl
from jax.experimental.pallas import tpu as pltpu
from jax.sharding import PartitionSpec as P

HEAD = 128
QPK = 8
SEQ_LEN = 1024
GROUP = 8
SKIP = 128
LIVE = SEQ_LEN - SKIP
MESH = pl.DeviceIdType.MESH
F32 = jnp.float32
BF16 = jnp.bfloat16
NT = (((1,), (1,)), ((), ()))
NN = (((1,), (0,)), ((), ()))


def flip(value, bits):
    for at in range(3):
        unit = 1 << at
        if bits & unit:
            value = value + unit - 2 * unit * lax.rem(lax.div(value, unit), 2)
    return value


def dot(a, b, dims):
    return lax.dot_general(a, b, dims, preferred_element_type=F32)


def kernel(
    layer_ref,
    cot_ref,
    vw_ref,
    rewards_ref,
    groups_ref,
    prompts_ref,
    step_ref,
    query_ref,
    kw_ref,
    ck_ref,
    cv_ref,
    len_ref,
    grad_ref,
    nk_ref,
    nv_ref,
    att_ref,
    layer_v,
    cot_v,
    vw_v,
    step_v,
    query_v,
    kw_v,
    ck_v,
    cv_v,
    flat_v,
    xall_v,
    wall_v,
    a_v,
    away_v,
    home_v,
    core_v,
    recv_v,
    att_v,
    load_sem,
    x_send,
    x_recv,
    xp_send,
    xp_recv,
    w_send,
    w_recv,
    pair_send,
    pair_recv,
    core_send,
    core_recv,
    rs_send,
    rs_recv,
    ready_sem,
):
    sec = lax.axis_index("sec")
    fs = lax.axis_index("fsdp")
    tp = lax.axis_index("tp")
    core = lax.rem(fs, 2)
    group = sec * 4 + fs
    seqs = layer_ref.shape[0] // SEQ_LEN
    n_seq = rewards_ref.shape[0]
    cols = layer_ref.shape[1]

    def device(q, dc, dt):
        return (flip(sec, q // 2), flip(fs, (q % 2) * 2 + dc), flip(tp, dt))

    def near(q):
        return 4 * (q % 2)

    barrier = pltpu.get_barrier_semaphore()
    for q in (4, 5, 2, 3, 6, 7, 1):
        pl.semaphore_signal(barrier, inc=1, device_id=device(q, 0, near(q)), device_id_type=MESH)
    pl.semaphore_signal(barrier, inc=1, device_id=device(0, 1, 0), device_id_type=MESH)
    for dt in range(1, 8):
        pl.semaphore_signal(barrier, inc=1, device_id=device(0, 0, dt), device_id_type=MESH)

    def load(src, dst, at):
        copy = pltpu.make_async_copy(src, dst, load_sem.at[at])
        copy.start()
        return copy

    step_load = load(step_ref, step_v, 0)
    vw_load = load(vw_ref, vw_v, 1)
    query_load = load(query_ref, query_v, 2)
    kw_load = load(kw_ref, kw_v, 3)
    rows_n = ck_ref.shape[0]
    ck_loads = [load(ck_ref.at[r], ck_v.at[r], 4 + r) for r in range(rows_n)]
    cv_loads = [load(cv_ref.at[r], cv_v.at[r], 8 + r) for r in range(rows_n)]
    cot_loads = [
        load(cot_ref.at[pl.ds(s * SEQ_LEN + SKIP, LIVE)], cot_v.at[pl.ds(s * LIVE, LIVE)], 12 + s)
        for s in range(seqs)
    ]
    layer_loads = [
        load(layer_ref.at[pl.ds(s * SEQ_LEN + SKIP, LIVE)], layer_v.at[pl.ds(s * LIVE, LIVE)], 16 + s)
        for s in range(seqs)
    ]

    first = group * seqs
    own_groups = [groups_ref[first + s] for s in range(seqs)]
    own_prompts = [prompts_ref[first + s] for s in range(seqs)]

    def scan(j, carry):
        prompts = carry[0] + prompts_ref[j]
        reward = rewards_ref[j]
        sums = [
            c + jnp.where(groups_ref[j] == g, reward, F32(0.0))
            for c, g in zip(carry[1:], own_groups)
        ]
        return (prompts, *sums)

    scanned = lax.fori_loop(0, n_seq, scan, (jnp.int32(0),) + (F32(0.0),) * seqs)
    responses = (n_seq * SEQ_LEN - scanned[0]).astype(F32)
    advantage = [rewards_ref[first + s] - scanned[1 + s] / F32(GROUP) for s in range(seqs)]

    step_load.wait()
    flat_v[...] = jnp.concatenate(
        [step_v[s].astype(F32) for s in range(step_v.shape[0])], axis=0
    ).astype(BF16)
    xall_v[0] = flat_v[:, pl.ds(pl.multiple_of(tp * cols, 128), cols)]
    vw_load.wait()
    row_at = sec * 2 + lax.div(fs, 2)
    wall_v[row_at, core] = vw_v[...]

    kw_load.wait()
    new_keys = dot(flat_v[...], kw_v[...], NT).astype(BF16)
    nk_ref[...] = new_keys

    pl.semaphore_wait(barrier, 15)
    for q in (4, 5, 2, 3, 6, 7, 1):
        at = pl.multiple_of(flip(tp, near(q)) * cols, 128)
        pltpu.make_async_remote_copy(
            src_ref=flat_v.at[:, pl.ds(at, cols)],
            dst_ref=xall_v.at[q],
            send_sem=x_send,
            recv_sem=x_recv,
            device_id=device(q, 0, near(q)),
            device_id_type=MESH,
        ).start()
    for dt in range(1, 8):
        pl.semaphore_signal(ready_sem, inc=1, device_id=device(0, 0, dt), device_id_type=MESH)

    def send_weight(q):
        pltpu.make_async_remote_copy(
            src_ref=vw_v,
            dst_ref=wall_v.at[row_at, core],
            send_sem=w_send,
            recv_sem=w_recv,
            device_id=device(q, 0, 0),
            device_id_type=MESH,
        ).start()

    for q in (4, 2, 6):
        send_weight(q)

    query_load.wait()
    steps_n = query_v.shape[0]
    q16 = jnp.concatenate([query_v[s].astype(F32) for s in range(steps_n)], axis=0).astype(BF16)
    stacked = jnp.concatenate([q16[:, h * HEAD : (h + 1) * HEAD] for h in range(QPK)], axis=0)
    n_q = QPK * steps_n * rows_n
    to_r = lax.broadcasted_iota(jnp.int32, (n_q, n_q), 0)
    frm = lax.broadcasted_iota(jnp.int32, (n_q, n_q), 1)
    per = steps_n * QPK
    src_of = lax.rem(to_r, QPK) * 16 + lax.rem(lax.div(to_r, QPK), steps_n) * rows_n + lax.div(to_r, per)
    perm = (frm == src_of).astype(F32).astype(BF16)
    scale = F32(1.0 / HEAD**0.5)
    queries = dot(perm, stacked, NN).astype(BF16)
    fresh = dot(queries, new_keys, NT) * scale
    i_at = lax.broadcasted_iota(jnp.int32, fresh.shape, 0)
    j_at = lax.broadcasted_iota(jnp.int32, fresh.shape, 1)
    causal = (lax.div(i_at, per) == lax.rem(j_at, rows_n)) & (
        lax.div(j_at, rows_n) <= lax.rem(lax.div(i_at, QPK), steps_n)
    )
    fresh = jnp.where(causal, fresh, F32(-1e30))
    fresh_top = jnp.max(fresh, axis=1, keepdims=True)
    slots = ck_v.shape[1]
    slot_at = lax.broadcasted_iota(jnp.int32, (per, slots), 1)
    fresh_probs = []
    for r in range(rows_n):
        part = slice(r * per, (r + 1) * per)
        ck_loads[r].wait()
        scores = dot(queries[part], ck_v[r], NT) * scale
        live = slot_at < len_ref[r]
        scores = jnp.where(live, scores, F32(-1e30))
        top = jnp.maximum(jnp.max(scores, axis=1, keepdims=True), fresh_top[part])
        e = jnp.where(live, jnp.exp(scores - top), F32(0.0))
        fe = jnp.where(causal[part], jnp.exp(fresh[part] - top), F32(0.0))
        total = jnp.sum(e, axis=1, keepdims=True) + jnp.sum(fe, axis=1, keepdims=True)
        inv = F32(1.0) / total
        cv_loads[r].wait()
        att_v[part, :] = dot((e * inv).astype(BF16), cv_v[r], NN)
        fresh_probs.append((fe * inv).astype(BF16).astype(F32))
    fresh_prob = jnp.concatenate(fresh_probs, axis=0).astype(BF16)

    pl.semaphore_wait(ready_sem, 7)
    for q in (5, 3, 7, 1):
        send_weight(q)

    rows_at = lax.broadcasted_iota(jnp.int32, (128, 128), 0)
    wide = cot_v.shape[1]
    for s in range(seqs):
        cot_loads[s].wait()
        if s == seqs - 1:
            pltpu.make_async_copy(xall_v.at[pl.ds(1, 7)], xall_v.at[pl.ds(1, 7)], x_recv).wait()
            x_pair = pltpu.make_async_remote_copy(
                src_ref=xall_v.at[pl.ds(0, 8)],
                dst_ref=xall_v.at[pl.ds(8, 8)],
                send_sem=xp_send,
                recv_sem=xp_recv,
                device_id=device(0, 1, 0),
                device_id_type=MESH,
            )
            x_pair.start()

        def weigh(j, _, s=s):
            at = pl.multiple_of(s * LIVE + j * 128, 128)
            weight = jnp.where(rows_at + (SKIP + j * 128) >= own_prompts[s], advantage[s], F32(0.0))
            for n in range(wide // 128):
                span = slice(n * 128, (n + 1) * 128)
                cot_v[pl.ds(at, 128), span] = (cot_v[pl.ds(at, 128), span].astype(F32) * weight).astype(BF16)
            return 0

        lax.fori_loop(0, LIVE // 128, weigh, 0)

    x_pair.wait_recv()
    x_all = xall_v[...].reshape(256, cols)
    for copy in layer_loads:
        copy.wait()
    tokens = layer_v.shape[0]
    blk = 512

    def outer(j, _):
        at = pl.multiple_of(j * blk, blk)
        a_v[:, pl.ds(at, blk)] = dot(xall_v[...].reshape(256, cols), layer_v[pl.ds(at, blk), :], NT).astype(BF16)
        return 0

    lax.fori_loop(0, tokens // blk, outer, 0)

    inv_resp = F32(1.0) / responses
    own = dot(x_all, jnp.concatenate([vw_v[...]] * 4, axis=0), NT)
    quarter = lax.div(lax.broadcasted_iota(jnp.int32, (256, 256), 1), 64)
    own = jnp.where(quarter == lax.rem(group, 4), own, F32(0.0))
    own_chunk = lax.div(group, 4)
    tp_hi, tp_lo = lax.div(tp, 2), lax.rem(tp, 2)
    copies = []

    def scatter(k):
        copies[k].wait_recv()
        home_v[k] = home_v[k] + core_v[k]
        for e in range(2):
            j = flip(tp_lo, e)
            dt = 2 * k + e
            for q in range(8):
                if q or dt:
                    pltpu.make_async_remote_copy(
                        src_ref=home_v.at[k, j, pl.ds(q * 16, 16)],
                        dst_ref=recv_v.at[q * 8 + dt],
                        send_sem=rs_send,
                        recv_sem=rs_recv,
                        device_id=device(q, 0, dt),
                        device_id_type=MESH,
                    ).start()
        if k == 0:
            recv_v[0] = home_v[0, tp_lo, 0:16, :]

    for k in range(4):
        at = flip(tp_hi, k)
        weighted = cot_v[:, pl.ds(pl.multiple_of(at * 256, 256), 256)]
        part = jnp.where(own_chunk == at, own, F32(0.0)) - dot(a_v[...], weighted, NN) * inv_resp
        for j in range(2):
            home_v[k, j] = part[:128, j * 128 : (j + 1) * 128]
            away_v[k, j] = part[128:, j * 128 : (j + 1) * 128]
        copy = pltpu.make_async_remote_copy(
            src_ref=away_v.at[k],
            dst_ref=core_v.at[k],
            send_sem=core_send.at[k],
            recv_sem=core_recv.at[k],
            device_id=device(0, 1, 0),
            device_id_type=MESH,
        )
        copy.start()
        copies.append(copy)
        if k:
            scatter(k - 1)
    scatter(3)

    pltpu.make_async_copy(wall_v.at[pl.ds(0, 7), 0], wall_v.at[pl.ds(0, 7), 0], w_recv).wait()
    pair = pltpu.make_async_remote_copy(
        src_ref=wall_v.at[:, core],
        dst_ref=wall_v.at[:, core],
        send_sem=pair_send,
        recv_sem=pair_recv,
        device_id=device(0, 1, 0),
        device_id_type=MESH,
    )
    pair.start()

    pair.wait()
    half = LIVE // 2

    def grad(j, _):
        at = pl.multiple_of(j * half, half)
        grad_ref[pl.ds(at, half), :] = dot(
            cot_v[pl.ds(at, half), :], wall_v[...].reshape(wide, cols), NN
        ).astype(BF16)
        return 0

    lax.fori_loop(0, tokens // half, grad, 0)

    pltpu.make_async_copy(recv_v.at[pl.ds(1, 63)], recv_v.at[pl.ds(1, 63)], rs_recv).wait()
    new_values = jnp.sum(recv_v[...], axis=0).astype(BF16)
    nv_ref[...] = new_values
    done = (att_v[...] + dot(fresh_prob, new_values, NN)).astype(BF16)
    back = dot(perm, done, (((0,), (0,)), ((), ()))).astype(BF16)
    for h in range(QPK):
        att_ref[:, h * HEAD : (h + 1) * HEAD] = back[h * 16 : (h + 1) * 16]

    pltpu.make_async_copy(recv_v.at[pl.ds(1, 63)], recv_v.at[pl.ds(1, 63)], rs_send).wait()
    pltpu.make_async_copy(xall_v.at[pl.ds(1, 7)], xall_v.at[pl.ds(1, 7)], x_send).wait()
    x_pair.wait_send()
    pltpu.make_async_copy(wall_v.at[pl.ds(0, 7), 0], wall_v.at[pl.ds(0, 7), 0], w_send).wait()
    for copy in copies:
        copy.wait_send()


def finish(held_ref, nk_ref, nv_ref, att_ref, grad_ref, nk_out, nv_out, att_out, zero_v, sem, zero_sem):
    seqs = held_ref.shape[0] // LIVE
    copies = [
        pltpu.make_async_copy(
            held_ref.at[pl.ds(s * LIVE, LIVE)],
            grad_ref.at[pl.ds(s * SEQ_LEN + SKIP, LIVE)],
            sem.at[s],
        )
        for s in range(seqs)
    ]
    for copy in copies:
        copy.start()
    zero_v[...] = jnp.zeros_like(zero_v)
    zeros = [
        pltpu.make_async_copy(zero_v, grad_ref.at[pl.ds(s * SEQ_LEN, SKIP)], zero_sem.at[s])
        for s in range(seqs)
    ]
    for copy in zeros:
        copy.start()
    rows_n = nk_out.shape[1]
    for src, dst in ((nk_ref, nk_out), (nv_ref, nv_out), (att_ref, att_out)):
        value = src[...].astype(F32)
        for s in range(dst.shape[0]):
            dst[s] = value[s * rows_n : (s + 1) * rows_n].astype(BF16)
    for copy in copies + zeros:
        copy.wait()


def body(*args):
    layer, cot, vw, rewards, groups, prompts, step, query, kw, ck, cv, lengths = args
    steps_n, rows_n, width = step.shape
    n = steps_n * rows_n
    seqs = layer.shape[0] // SEQ_LEN
    tokens = seqs * LIVE
    cols = layer.shape[1]
    hbm = pl.BlockSpec(memory_space=pl.ANY)
    smem = pl.BlockSpec(memory_space=pltpu.SMEM)
    vmem = pl.BlockSpec(memory_space=pltpu.VMEM)
    dma = pltpu.SemaphoreType.DMA
    grad, new_keys, new_values, attended = pl.pallas_call(
        kernel,
        out_shape=(
            pltpu.VMEM((tokens, cols), BF16),
            pltpu.VMEM((n, HEAD), BF16),
            pltpu.VMEM((n, HEAD), BF16),
            pltpu.VMEM((n, QPK * HEAD), BF16),
        ),
        in_specs=[hbm, hbm, hbm, smem, smem, smem, hbm, hbm, hbm, hbm, hbm, smem],
        out_specs=(vmem,) * 4,
        scratch_shapes=[
            pltpu.VMEM((tokens, cols), BF16),
            pltpu.VMEM((tokens, cot.shape[1]), BF16),
            pltpu.VMEM(vw.shape, BF16),
            pltpu.VMEM(step.shape, BF16),
            pltpu.VMEM(query.shape, BF16),
            pltpu.VMEM(kw.shape, BF16),
            pltpu.VMEM(ck.shape, BF16),
            pltpu.VMEM(cv.shape, BF16),
            pltpu.VMEM((n, width), BF16),
            pltpu.VMEM((16, n, cols), BF16),
            pltpu.VMEM((8, 2, *vw.shape), BF16),
            pltpu.VMEM((256, tokens), BF16),
            pltpu.VMEM((4, 2, 128, 128), F32),
            pltpu.VMEM((4, 2, 128, 128), F32),
            pltpu.VMEM((4, 2, 128, 128), F32),
            pltpu.VMEM((64, n, HEAD), F32),
            pltpu.VMEM((128, HEAD), F32),
            dma((20,)),
            dma,
            dma,
            dma,
            dma,
            dma,
            dma,
            dma,
            dma,
            dma((4,)),
            dma((4,)),
            dma,
            dma,
            pltpu.SemaphoreType.REGULAR,
        ],
        compiler_params=pltpu.CompilerParams(
            collective_id=0, has_side_effects=True, vmem_limit_bytes=56 * 1024 * 1024
        ),
    )(*(pltpu.with_memory_space_constraint(v, pltpu.HBM) if v.dtype == BF16 else v for v in args))
    held = [pltpu.with_memory_space_constraint(v, pltpu.VMEM) for v in (grad, new_keys, new_values, attended)]
    return pl.pallas_call(
        finish,
        out_shape=(
            jax.ShapeDtypeStruct(layer.shape, BF16),
            jax.ShapeDtypeStruct((steps_n, rows_n, HEAD), BF16),
            jax.ShapeDtypeStruct((steps_n, rows_n, HEAD), BF16),
            jax.ShapeDtypeStruct((steps_n, rows_n, QPK * HEAD), BF16),
        ),
        in_specs=[vmem] * 4,
        out_specs=(hbm, vmem, vmem, vmem),
        scratch_shapes=[
            pltpu.VMEM((SKIP, cols), BF16),
            dma((seqs,)),
            dma((seqs,)),
        ],
        compiler_params=pltpu.CompilerParams(vmem_limit_bytes=8 * 1024 * 1024),
    )(*held)


def solution(mesh):
    tokens = ("sec", "fsdp")
    in_specs = (
        P(tokens, "tp"),
        P(tokens, None),
        P(tokens, "tp"),
        P(),
        P(),
        P(),
        P(None, tokens, None),
        P(None, tokens, "tp"),
        P("tp", None),
        P(tokens, None, "tp"),
        P(tokens, None, "tp"),
        P(tokens),
    )
    out_specs = (
        P(tokens, "tp"),
        P(None, tokens, "tp"),
        P(None, tokens, "tp"),
        P(None, tokens, "tp"),
    )
    return jax.shard_map(body, mesh=mesh, in_specs=in_specs, out_specs=out_specs, check_vma=False)
```

```python
import functools

import jax
import jax.numpy as jnp
from jax import lax
from jax.experimental import pallas as pl
from jax.experimental.pallas import tpu as pltpu
from jax.sharding import PartitionSpec as P

HEAD = 128
QPK = 8
SEQ_LEN = 1024
GROUP = 8
SKIP = 128
LIVE = SEQ_LEN - SKIP
MESH = pl.DeviceIdType.MESH
F32 = jnp.float32
BF16 = jnp.bfloat16
NT = (((1,), (1,)), ((), ()))
NN = (((1,), (0,)), ((), ()))


def flip(value, bits):
    for at in range(3):
        unit = 1 << at
        if bits & unit:
            value = value + unit - 2 * unit * lax.rem(lax.div(value, unit), 2)
    return value


def dot(a, b, dims):
    return lax.dot_general(a, b, dims, preferred_element_type=F32)


def kernel(
    layer_ref,
    cot_ref,
    vw_ref,
    rewards_ref,
    groups_ref,
    prompts_ref,
    step_ref,
    query_ref,
    kw_ref,
    ck_ref,
    cv_ref,
    len_ref,
    grad_ref,
    nk_ref,
    nv_ref,
    att_ref,
    fresh_ref,
    perm_ref,
    layer_v,
    cot_v,
    vw_v,
    step_v,
    query_v,
    kw_v,
    ck_v,
    cv_v,
    flat_v,
    xall_v,
    wall_v,
    a_v,
    away_v,
    home_v,
    core_v,
    recv_v,
    load_sem,
    x_send,
    x_recv,
    xp_send,
    xp_recv,
    w_send,
    w_recv,
    pair_send,
    pair_recv,
    core_send,
    core_recv,
    rs_send,
    rs_recv,
    ready_sem,
):
    sec = lax.axis_index("sec")
    fs = lax.axis_index("fsdp")
    tp = lax.axis_index("tp")
    core = lax.rem(fs, 2)
    yh = lax.div(fs, 2)
    group = sec * 4 + fs
    seqs = layer_ref.shape[0] // SEQ_LEN
    n_seq = rewards_ref.shape[0]
    cols = layer_ref.shape[1]

    def device(q, dc, dt):
        return (flip(sec, q // 2), flip(fs, (q % 2) * 2 + dc), flip(tp, dt))

    def near(q):
        return 4 * (q % 2)

    barrier = pltpu.get_barrier_semaphore()
    for q in (4, 5, 2, 3, 6, 7, 1):
        pl.semaphore_signal(barrier, inc=1, device_id=device(q, 0, near(q)), device_id_type=MESH)
    pl.semaphore_signal(barrier, inc=1, device_id=device(0, 1, 0), device_id_type=MESH)
    for dt in range(1, 8):
        pl.semaphore_signal(barrier, inc=1, device_id=device(0, 0, dt), device_id_type=MESH)

    def load(src, dst, at):
        copy = pltpu.make_async_copy(src, dst, load_sem.at[at])
        copy.start()
        return copy

    step_load = load(step_ref, step_v, 0)
    vw_load = load(vw_ref, vw_v, 1)
    query_load = load(query_ref, query_v, 2)
    kw_load = load(kw_ref, kw_v, 3)
    rows_n = ck_ref.shape[0]
    ck_loads = [load(ck_ref.at[r], ck_v.at[r], 4 + r) for r in range(rows_n)]
    cv_loads = [load(cv_ref.at[r], cv_v.at[r], 8 + r) for r in range(rows_n)]
    cot_loads = [
        load(cot_ref.at[pl.ds(s * SEQ_LEN + SKIP, LIVE)], cot_v.at[pl.ds(s * LIVE, LIVE)], 12 + s)
        for s in range(seqs)
    ]
    layer_loads = [
        load(layer_ref.at[pl.ds(s * SEQ_LEN + SKIP, LIVE)], layer_v.at[pl.ds(s * LIVE, LIVE)], 16 + s)
        for s in range(seqs)
    ]

    first = group * seqs
    own_groups = [groups_ref[first + s] for s in range(seqs)]
    own_prompts = [prompts_ref[first + s] for s in range(seqs)]

    def scan(j, carry):
        prompts = carry[0] + prompts_ref[j]
        reward = rewards_ref[j]
        sums = [
            c + jnp.where(groups_ref[j] == g, reward, F32(0.0))
            for c, g in zip(carry[1:], own_groups)
        ]
        return (prompts, *sums)

    scanned = lax.fori_loop(0, n_seq, scan, (jnp.int32(0),) + (F32(0.0),) * seqs)
    responses = (n_seq * SEQ_LEN - scanned[0]).astype(F32)
    advantage = [rewards_ref[first + s] - scanned[1 + s] / F32(GROUP) for s in range(seqs)]

    step_load.wait()
    flat_v[...] = jnp.concatenate(
        [step_v[s].astype(F32) for s in range(step_v.shape[0])], axis=0
    ).astype(BF16)
    xall_v[0] = flat_v[:, pl.ds(pl.multiple_of(tp * cols, 128), cols)]
    vw_load.wait()
    wall_v[sec, yh, core] = vw_v[...]

    kw_load.wait()
    new_keys = dot(flat_v[...], kw_v[...], NT).astype(BF16)
    nk_ref[...] = new_keys

    pl.semaphore_wait(barrier, 15)
    for q in (4, 5, 2, 3, 6, 7, 1):
        at = pl.multiple_of(flip(tp, near(q)) * cols, 128)
        pltpu.make_async_remote_copy(
            src_ref=flat_v.at[:, pl.ds(at, cols)],
            dst_ref=xall_v.at[q],
            send_sem=x_send,
            recv_sem=x_recv,
            device_id=device(q, 0, near(q)),
            device_id_type=MESH,
        ).start()
    for dt in range(1, 8):
        pl.semaphore_signal(ready_sem, inc=1, device_id=device(0, 0, dt), device_id_type=MESH)

    def send_weight(q):
        pltpu.make_async_remote_copy(
            src_ref=vw_v,
            dst_ref=wall_v.at[sec, yh, core],
            send_sem=w_send.at[q % 2],
            recv_sem=w_recv.at[q % 2],
            device_id=device(q, 0, 0),
            device_id_type=MESH,
        ).start()

    for q in (4, 2, 6):
        send_weight(q)

    query_load.wait()
    steps_n = query_v.shape[0]
    q16 = jnp.concatenate([query_v[s].astype(F32) for s in range(steps_n)], axis=0).astype(BF16)
    stacked = jnp.concatenate([q16[:, h * HEAD : (h + 1) * HEAD] for h in range(QPK)], axis=0)
    n_q = QPK * steps_n * rows_n
    to_r = lax.broadcasted_iota(jnp.int32, (n_q, n_q), 0)
    frm = lax.broadcasted_iota(jnp.int32, (n_q, n_q), 1)
    per = steps_n * QPK
    src_of = lax.rem(to_r, QPK) * 16 + lax.rem(lax.div(to_r, QPK), steps_n) * rows_n + lax.div(to_r, per)
    perm = (frm == src_of).astype(F32).astype(BF16)
    scale = F32(1.0 / HEAD**0.5)
    queries = dot(perm, stacked, NN).astype(BF16)
    fresh = dot(queries, new_keys, NT) * scale
    i_at = lax.broadcasted_iota(jnp.int32, fresh.shape, 0)
    j_at = lax.broadcasted_iota(jnp.int32, fresh.shape, 1)
    causal = (lax.div(i_at, per) == lax.rem(j_at, rows_n)) & (
        lax.div(j_at, rows_n) <= lax.rem(lax.div(i_at, QPK), steps_n)
    )
    fresh = jnp.where(causal, fresh, F32(-1e30))
    fresh_top = jnp.max(fresh, axis=1, keepdims=True)
    slots = ck_v.shape[1]
    slot_at = lax.broadcasted_iota(jnp.int32, (per, slots), 1)
    fresh_probs = []
    for r in range(rows_n):
        part = slice(r * per, (r + 1) * per)
        ck_loads[r].wait()
        scores = dot(queries[part], ck_v[r], NT) * scale
        live = slot_at < len_ref[r]
        scores = jnp.where(live, scores, F32(-1e30))
        top = jnp.maximum(jnp.max(scores, axis=1, keepdims=True), fresh_top[part])
        e = jnp.where(live, jnp.exp(scores - top), F32(0.0))
        fe = jnp.where(causal[part], jnp.exp(fresh[part] - top), F32(0.0))
        total = jnp.sum(e, axis=1, keepdims=True) + jnp.sum(fe, axis=1, keepdims=True)
        inv = F32(1.0) / total
        cv_loads[r].wait()
        att_ref[part, :] = dot((e * inv).astype(BF16), cv_v[r], NN)
        fresh_probs.append((fe * inv).astype(BF16).astype(F32))
    fresh_ref[...] = jnp.concatenate(fresh_probs, axis=0).astype(BF16)
    perm_ref[...] = perm

    pl.semaphore_wait(ready_sem, 7)
    for q in (5, 3, 7, 1):
        send_weight(q)

    rows_at = lax.broadcasted_iota(jnp.int32, (128, 128), 0)
    wide = cot_v.shape[1]
    for s in range(seqs):
        cot_loads[s].wait()
        if s == seqs - 1:
            pltpu.make_async_copy(xall_v.at[pl.ds(1, 7)], xall_v.at[pl.ds(1, 7)], x_recv).wait()
            x_pair = pltpu.make_async_remote_copy(
                src_ref=xall_v.at[pl.ds(0, 8)],
                dst_ref=xall_v.at[pl.ds(8, 8)],
                send_sem=xp_send,
                recv_sem=xp_recv,
                device_id=device(0, 1, 0),
                device_id_type=MESH,
            )
            x_pair.start()

        def weigh(j, _, s=s):
            at = pl.multiple_of(s * LIVE + j * 128, 128)
            weight = jnp.where(rows_at + (SKIP + j * 128) >= own_prompts[s], advantage[s], F32(0.0))
            for n in range(wide // 128):
                span = slice(n * 128, (n + 1) * 128)
                cot_v[pl.ds(at, 128), span] = (cot_v[pl.ds(at, 128), span].astype(F32) * weight).astype(BF16)
            return 0

        lax.fori_loop(0, LIVE // 128, weigh, 0)

    x_pair.wait_recv()
    x_all = xall_v[...].reshape(256, cols)
    tokens = layer_v.shape[0]
    blk = LIVE

    for j in range(tokens // blk):
        layer_loads[j].wait()
        a_v[:, j * blk : (j + 1) * blk] = dot(x_all, layer_v[j * blk : (j + 1) * blk, :], NT).astype(BF16)

    def pass_on(batch):
        half_at = flip(yh, batch)
        n = 3 + batch
        pltpu.make_async_copy(wall_v.at[pl.ds(0, n), 0, 0], wall_v.at[pl.ds(0, n), 0, 0], w_recv.at[batch]).wait()
        copy = pltpu.make_async_remote_copy(
            src_ref=wall_v.at[:, half_at, core],
            dst_ref=wall_v.at[:, half_at, core],
            send_sem=pair_send.at[batch],
            recv_sem=pair_recv.at[batch],
            device_id=device(0, 1, 0),
            device_id_type=MESH,
        )
        copy.start()
        return copy

    pairs = [pass_on(0)]

    inv_resp = F32(1.0) / responses
    own = dot(x_all, jnp.concatenate([vw_v[...]] * 4, axis=0), NT)
    quarter = lax.div(lax.broadcasted_iota(jnp.int32, (256, 256), 1), 64)
    own = jnp.where(quarter == lax.rem(group, 4), own, F32(0.0))
    own_chunk = lax.div(group, 4)
    tp_hi, tp_lo = lax.div(tp, 2), lax.rem(tp, 2)
    copies = {}

    def scatter(k):
        copies[k].wait_recv()
        home_v[k] = home_v[k] + core_v[k]
        for e in (0, 1) if k == 1 else (1, 0):
            j = flip(tp_lo, e)
            dt = 2 * k + e
            for q in (5, 3, 7, 4, 1, 2, 6, 0):
                if q or dt:
                    pltpu.make_async_remote_copy(
                        src_ref=home_v.at[k, j, pl.ds(q * 16, 16)],
                        dst_ref=recv_v.at[q * 8 + dt],
                        send_sem=rs_send,
                        recv_sem=rs_recv,
                        device_id=device(q, 0, dt),
                        device_id_type=MESH,
                    ).start()
        if k == 0:
            recv_v[0] = home_v[0, tp_lo, 0:16, :]

    last = None
    for k in (3, 1, 2, 0):
        at = flip(tp_hi, k)
        weighted = cot_v[:, pl.ds(pl.multiple_of(at * 256, 256), 256)]
        part = jnp.where(own_chunk == at, own, F32(0.0)) - dot(a_v[...], weighted, NN) * inv_resp
        for j in range(2):
            home_v[k, j] = part[:128, j * 128 : (j + 1) * 128]
            away_v[k, j] = part[128:, j * 128 : (j + 1) * 128]
        copies[k] = pltpu.make_async_remote_copy(
            src_ref=away_v.at[k],
            dst_ref=core_v.at[k],
            send_sem=core_send.at[k],
            recv_sem=core_recv.at[k],
            device_id=device(0, 1, 0),
            device_id_type=MESH,
        )
        copies[k].start()
        if last is not None:
            scatter(last)
        last = k
    pairs.append(pass_on(1))
    scatter(last)

    for copy in pairs:
        copy.wait()
    half = 2 * LIVE

    def grad(j, _):
        at = pl.multiple_of(j * half, half)
        grad_ref[pl.ds(at, half), :] = dot(
            cot_v[pl.ds(at, half), :], wall_v[...].reshape(wide, cols), NN
        ).astype(BF16)
        return 0

    lax.fori_loop(0, tokens // half, grad, 0)

    pltpu.make_async_copy(recv_v.at[pl.ds(1, 63)], recv_v.at[pl.ds(1, 63)], rs_recv).wait()
    new_values = jnp.sum(recv_v[...], axis=0).astype(BF16)
    nv_ref[...] = new_values

    pltpu.make_async_copy(recv_v.at[pl.ds(1, 63)], recv_v.at[pl.ds(1, 63)], rs_send).wait()
    pltpu.make_async_copy(xall_v.at[pl.ds(1, 7)], xall_v.at[pl.ds(1, 7)], x_send).wait()
    x_pair.wait_send()
    for n in (3, 4):
        pltpu.make_async_copy(wall_v.at[pl.ds(0, n), 0, 0], wall_v.at[pl.ds(0, n), 0, 0], w_send.at[n - 3]).wait()
    for k in range(4):
        copies[k].wait_send()


def finish(held_ref, nk_ref, nv_ref, att_ref, fresh_ref, perm_ref, grad_ref, nk_out, nv_out, att_out, zero_v, sem, zero_sem):
    seqs = held_ref.shape[0] // LIVE
    copies = [
        pltpu.make_async_copy(
            held_ref.at[pl.ds(s * LIVE, LIVE)],
            grad_ref.at[pl.ds(s * SEQ_LEN + SKIP, LIVE)],
            sem.at[s],
        )
        for s in range(seqs)
    ]
    for copy in copies:
        copy.start()
    zero_v[...] = jnp.zeros_like(zero_v)
    zeros = [
        pltpu.make_async_copy(zero_v, grad_ref.at[pl.ds(s * SEQ_LEN, SKIP)], zero_sem.at[s])
        for s in range(seqs)
    ]
    for copy in zeros:
        copy.start()
    rows_n = nk_out.shape[1]
    done = (att_ref[...] + dot(fresh_ref[...], nv_ref[...], NN)).astype(BF16)
    back = dot(perm_ref[...], done, (((0,), (0,)), ((), ())))
    attended = jnp.concatenate([back[h * 16 : (h + 1) * 16] for h in range(QPK)], axis=1)
    for value, dst in (
        (nk_ref[...].astype(F32), nk_out),
        (nv_ref[...].astype(F32), nv_out),
        (attended, att_out),
    ):
        for s in range(dst.shape[0]):
            dst[s] = value[s * rows_n : (s + 1) * rows_n].astype(BF16)
    for copy in copies + zeros:
        copy.wait()


def body(*args):
    layer, cot, vw, rewards, groups, prompts, step, query, kw, ck, cv, lengths = args
    steps_n, rows_n, width = step.shape
    n = steps_n * rows_n
    seqs = layer.shape[0] // SEQ_LEN
    tokens = seqs * LIVE
    cols = layer.shape[1]
    hbm = pl.BlockSpec(memory_space=pl.ANY)
    smem = pl.BlockSpec(memory_space=pltpu.SMEM)
    vmem = pl.BlockSpec(memory_space=pltpu.VMEM)
    dma = pltpu.SemaphoreType.DMA
    results = pl.pallas_call(
        kernel,
        out_shape=(
            pltpu.VMEM((tokens, cols), BF16),
            pltpu.VMEM((n, HEAD), BF16),
            pltpu.VMEM((n, HEAD), BF16),
            pltpu.VMEM((n * QPK, HEAD), F32),
            pltpu.VMEM((n * QPK, n), BF16),
            pltpu.VMEM((n * QPK, n * QPK), BF16),
        ),
        in_specs=[hbm, hbm, hbm, smem, smem, smem, hbm, hbm, hbm, hbm, hbm, smem],
        out_specs=(vmem,) * 6,
        scratch_shapes=[
            pltpu.VMEM((tokens, cols), BF16),
            pltpu.VMEM((tokens, cot.shape[1]), BF16),
            pltpu.VMEM(vw.shape, BF16),
            pltpu.VMEM(step.shape, BF16),
            pltpu.VMEM(query.shape, BF16),
            pltpu.VMEM(kw.shape, BF16),
            pltpu.VMEM(ck.shape, BF16),
            pltpu.VMEM(cv.shape, BF16),
            pltpu.VMEM((n, width), BF16),
            pltpu.VMEM((16, n, cols), BF16),
            pltpu.VMEM((4, 2, 2, *vw.shape), BF16),
            pltpu.VMEM((256, tokens), BF16),
            pltpu.VMEM((4, 2, 128, 128), F32),
            pltpu.VMEM((4, 2, 128, 128), F32),
            pltpu.VMEM((4, 2, 128, 128), F32),
            pltpu.VMEM((64, n, HEAD), F32),
            dma((20,)),
            dma,
            dma,
            dma,
            dma,
            dma((2,)),
            dma((2,)),
            dma((2,)),
            dma((2,)),
            dma((4,)),
            dma((4,)),
            dma,
            dma,
            pltpu.SemaphoreType.REGULAR,
        ],
        compiler_params=pltpu.CompilerParams(
            collective_id=0, has_side_effects=True, vmem_limit_bytes=56 * 1024 * 1024
        ),
    )(*(pltpu.with_memory_space_constraint(v, pltpu.HBM) if v.dtype == BF16 else v for v in args))
    held = [pltpu.with_memory_space_constraint(v, pltpu.VMEM) for v in results]
    return pl.pallas_call(
        finish,
        out_shape=(
            jax.ShapeDtypeStruct(layer.shape, BF16),
            jax.ShapeDtypeStruct((steps_n, rows_n, HEAD), BF16),
            jax.ShapeDtypeStruct((steps_n, rows_n, HEAD), BF16),
            jax.ShapeDtypeStruct((steps_n, rows_n, QPK * HEAD), BF16),
        ),
        in_specs=[vmem] * 6,
        out_specs=(hbm, vmem, vmem, vmem),
        scratch_shapes=[
            pltpu.VMEM((SKIP, cols), BF16),
            dma((seqs,)),
            dma((seqs,)),
        ],
        compiler_params=pltpu.CompilerParams(vmem_limit_bytes=8 * 1024 * 1024),
    )(*held)


def solution(mesh):
    tokens = ("sec", "fsdp")
    in_specs = (
        P(tokens, "tp"),
        P(tokens, None),
        P(tokens, "tp"),
        P(),
        P(),
        P(),
        P(None, tokens, None),
        P(None, tokens, "tp"),
        P("tp", None),
        P(tokens, None, "tp"),
        P(tokens, None, "tp"),
        P(tokens),
    )
    out_specs = (
        P(tokens, "tp"),
        P(None, tokens, "tp"),
        P(None, tokens, "tp"),
        P(None, tokens, "tp"),
    )
    return jax.shard_map(body, mesh=mesh, in_specs=in_specs, out_specs=out_specs, check_vma=False)
```

```python
import functools

import jax
import jax.numpy as jnp
from jax import lax
from jax.experimental import pallas as pl
from jax.experimental.pallas import tpu as pltpu
from jax.sharding import PartitionSpec as P

HEAD = 128
QPK = 8
SEQ_LEN = 1024
GROUP = 8
SKIP = 128
LIVE = SEQ_LEN - SKIP
MESH = pl.DeviceIdType.MESH
F32 = jnp.float32
BF16 = jnp.bfloat16
NT = (((1,), (1,)), ((), ()))
NN = (((1,), (0,)), ((), ()))


def flip(value, bits):
    for at in range(3):
        unit = 1 << at
        if bits & unit:
            value = value + unit - 2 * unit * lax.rem(lax.div(value, unit), 2)
    return value


def dot(a, b, dims):
    return lax.dot_general(a, b, dims, preferred_element_type=F32)


def kernel(
    layer_ref,
    cot_ref,
    vw_ref,
    rewards_ref,
    groups_ref,
    prompts_ref,
    step_ref,
    query_ref,
    kw_ref,
    ck_ref,
    cv_ref,
    len_ref,
    grad_ref,
    nk_ref,
    nv_ref,
    att_ref,
    fresh_ref,
    perm_ref,
    cot_v,
    wall_v,
    layer_v,
    vw_v,
    step_v,
    query_v,
    kw_v,
    ck_v,
    cv_v,
    flat_v,
    xall_v,
    a_v,
    away_v,
    home_v,
    core_v,
    recv_v,
    load_sem,
    x_send,
    x_recv,
    xp_send,
    xp_recv,
    w_send,
    w_recv,
    pair_send,
    pair_recv,
    core_send,
    core_recv,
    rs_send,
    rs_recv,
    ready_sem,
):
    sec = lax.axis_index("sec")
    fs = lax.axis_index("fsdp")
    tp = lax.axis_index("tp")
    core = lax.rem(fs, 2)
    yh = lax.div(fs, 2)
    group = sec * 4 + fs
    seqs = layer_ref.shape[0] // SEQ_LEN
    n_seq = rewards_ref.shape[0]
    cols = layer_ref.shape[1]

    def device(q, dc, dt):
        return (flip(sec, q // 2), flip(fs, (q % 2) * 2 + dc), flip(tp, dt))

    def near(q):
        return 4 * (q % 2)

    barrier = pltpu.get_barrier_semaphore()
    for q in (4, 5, 2, 3, 6, 7, 1):
        pl.semaphore_signal(barrier, inc=1, device_id=device(q, 0, near(q)), device_id_type=MESH)
    pl.semaphore_signal(barrier, inc=1, device_id=device(0, 1, 0), device_id_type=MESH)
    pl.semaphore_signal(barrier, inc=1, device_id=device(1, 0, 0), device_id_type=MESH)
    for dt in range(1, 8):
        pl.semaphore_signal(barrier, inc=1, device_id=device(0, 0, dt), device_id_type=MESH)

    def load(src, dst, at):
        copy = pltpu.make_async_copy(src, dst, load_sem.at[at])
        copy.start()
        return copy

    step_load = load(step_ref, step_v, 0)
    vw_load = load(vw_ref, vw_v, 1)
    query_load = load(query_ref, query_v, 2)
    kw_load = load(kw_ref, kw_v, 3)
    rows_n = ck_ref.shape[0]
    ck_loads = [load(ck_ref.at[r], ck_v.at[r], 4 + r) for r in range(rows_n)]
    cv_loads = [load(cv_ref.at[r], cv_v.at[r], 8 + r) for r in range(rows_n)]
    cot_loads = [
        load(cot_ref.at[pl.ds(s * SEQ_LEN + SKIP, LIVE)], cot_v.at[pl.ds(s * LIVE, LIVE)], 12 + s)
        for s in range(seqs)
    ]
    layer_loads = [
        load(layer_ref.at[pl.ds(s * SEQ_LEN + SKIP, LIVE)], layer_v.at[pl.ds(s * LIVE, LIVE)], 16 + s)
        for s in range(seqs)
    ]

    first = group * seqs
    own_groups = [groups_ref[first + s] for s in range(seqs)]
    own_prompts = [prompts_ref[first + s] for s in range(seqs)]

    def scan(j, carry):
        prompts = carry[0] + prompts_ref[j]
        reward = rewards_ref[j]
        sums = [
            c + jnp.where(groups_ref[j] == g, reward, F32(0.0))
            for c, g in zip(carry[1:], own_groups)
        ]
        return (prompts, *sums)

    scanned = lax.fori_loop(0, n_seq, scan, (jnp.int32(0),) + (F32(0.0),) * seqs)
    responses = (n_seq * SEQ_LEN - scanned[0]).astype(F32)
    advantage = [rewards_ref[first + s] - scanned[1 + s] / F32(GROUP) for s in range(seqs)]

    step_load.wait()
    flat_v[...] = jnp.concatenate(
        [step_v[s].astype(F32) for s in range(step_v.shape[0])], axis=0
    ).astype(BF16)
    xall_v[0] = flat_v[:, pl.ds(pl.multiple_of(tp * cols, 128), cols)]
    vw_load.wait()
    wall_v[sec, yh, core] = vw_v[...]

    kw_load.wait()
    new_keys = dot(flat_v[...], kw_v[...], NT).astype(BF16)
    nk_ref[...] = new_keys

    pl.semaphore_wait(barrier, 16)
    for q in (4, 5, 2, 3, 6, 7, 1):
        at = pl.multiple_of(flip(tp, near(q)) * cols, 128)
        pltpu.make_async_remote_copy(
            src_ref=flat_v.at[:, pl.ds(at, cols)],
            dst_ref=xall_v.at[q],
            send_sem=x_send,
            recv_sem=x_recv,
            device_id=device(q, 0, near(q)),
            device_id_type=MESH,
        ).start()
    for dt in range(1, 8):
        pl.semaphore_signal(ready_sem, inc=1, device_id=device(0, 0, dt), device_id_type=MESH)

    def send_weight(q, half_at, at):
        pltpu.make_async_remote_copy(
            src_ref=wall_v.at[sec, half_at, core],
            dst_ref=wall_v.at[sec, half_at, core],
            send_sem=w_send.at[at],
            recv_sem=w_recv.at[at],
            device_id=device(q, 0, 0),
            device_id_type=MESH,
        ).start()

    def weight_bytes(n):
        return wall_v.at[pl.ds(0, n), 0, 0]

    send_weight(1, yh, 2)
    for q in (4, 2, 6):
        send_weight(q, yh, 0)

    query_load.wait()
    steps_n = query_v.shape[0]
    q16 = jnp.concatenate([query_v[s].astype(F32) for s in range(steps_n)], axis=0).astype(BF16)
    stacked = jnp.concatenate([q16[:, h * HEAD : (h + 1) * HEAD] for h in range(QPK)], axis=0)
    n_q = QPK * steps_n * rows_n
    to_r = lax.broadcasted_iota(jnp.int32, (n_q, n_q), 0)
    frm = lax.broadcasted_iota(jnp.int32, (n_q, n_q), 1)
    per = steps_n * QPK
    src_of = lax.rem(to_r, QPK) * 16 + lax.rem(lax.div(to_r, QPK), steps_n) * rows_n + lax.div(to_r, per)
    perm = (frm == src_of).astype(F32).astype(BF16)
    scale = F32(1.0 / HEAD**0.5)
    queries = dot(perm, stacked, NN).astype(BF16)
    fresh = dot(queries, new_keys, NT) * scale
    i_at = lax.broadcasted_iota(jnp.int32, fresh.shape, 0)
    j_at = lax.broadcasted_iota(jnp.int32, fresh.shape, 1)
    causal = (lax.div(i_at, per) == lax.rem(j_at, rows_n)) & (
        lax.div(j_at, rows_n) <= lax.rem(lax.div(i_at, QPK), steps_n)
    )
    fresh = jnp.where(causal, fresh, F32(-1e30))
    fresh_top = jnp.max(fresh, axis=1, keepdims=True)
    slots = ck_v.shape[1]
    slot_at = lax.broadcasted_iota(jnp.int32, (per, slots), 1)
    for copy in ck_loads + cv_loads:
        copy.wait()
    parts = [slice(r * per, (r + 1) * per) for r in range(rows_n)]
    raw = [dot(queries[parts[r]], ck_v[r], NT) * scale for r in range(rows_n)]
    raw = [jnp.where(slot_at < len_ref[r], raw[r], F32(-1e30)) for r in range(rows_n)]
    tops = [jnp.maximum(jnp.max(raw[r], axis=1, keepdims=True), fresh_top[parts[r]]) for r in range(rows_n)]
    exps = [jnp.exp(raw[r] - tops[r]) for r in range(rows_n)]
    fresh_exps = [jnp.exp(fresh[parts[r]] - tops[r]) for r in range(rows_n)]
    fresh_probs = []
    for r in range(rows_n):
        total = jnp.sum(exps[r], axis=1, keepdims=True) + jnp.sum(fresh_exps[r], axis=1, keepdims=True)
        inv = F32(1.0) / total
        att_ref[parts[r], :] = dot((exps[r] * inv).astype(BF16), cv_v[r], NN)
        fresh_probs.append((fresh_exps[r] * inv).astype(BF16).astype(F32))
    fresh_ref[...] = jnp.concatenate(fresh_probs, axis=0).astype(BF16)
    perm_ref[...] = perm

    rows_at = lax.broadcasted_iota(jnp.int32, (128, 128), 0)
    wide = cot_v.shape[1]
    for s in range(seqs):
        cot_loads[s].wait()
        if s == seqs - 1:
            pltpu.make_async_copy(xall_v.at[pl.ds(1, 7)], xall_v.at[pl.ds(1, 7)], x_recv).wait()
            x_pair = pltpu.make_async_remote_copy(
                src_ref=xall_v.at[pl.ds(0, 8)],
                dst_ref=xall_v.at[pl.ds(8, 8)],
                send_sem=xp_send,
                recv_sem=xp_recv,
                device_id=device(0, 1, 0),
                device_id_type=MESH,
            )
            x_pair.start()

        def weigh(j, _, s=s):
            at = pl.multiple_of(s * LIVE + j * 128, 128)
            weight = jnp.where(rows_at + (SKIP + j * 128) >= own_prompts[s], advantage[s], F32(0.0))
            for n in range(wide // 128):
                span = slice(n * 128, (n + 1) * 128)
                cot_v[pl.ds(at, 128), span] = (cot_v[pl.ds(at, 128), span].astype(F32) * weight).astype(BF16)
            return 0

        lax.fori_loop(0, LIVE // 128, weigh, 0)

    def pass_on(batch):
        half_at = flip(yh, batch)
        pltpu.make_async_copy(weight_bytes(3), weight_bytes(3), w_recv.at[batch]).wait()
        copy = pltpu.make_async_remote_copy(
            src_ref=wall_v.at[:, half_at, core],
            dst_ref=wall_v.at[:, half_at, core],
            send_sem=pair_send.at[batch],
            recv_sem=pair_recv.at[batch],
            device_id=device(0, 1, 0),
            device_id_type=MESH,
        )
        copy.start()
        return copy

    inv_resp = F32(1.0) / responses
    quarter = lax.div(lax.broadcasted_iota(jnp.int32, (128, 256), 1), 64)
    own_chunk = lax.div(group, 4)
    tp_hi, tp_lo = lax.div(tp, 2), lax.rem(tp, 2)
    vw_four = jnp.concatenate([vw_v[...]] * 4, axis=0)

    def project(side):
        x = xall_v[side * 8 : side * 8 + 8].reshape(128, cols)
        for s in range(seqs):
            if not side:
                layer_loads[s].wait()
            span = slice(s * LIVE, (s + 1) * LIVE)
            a_v[side * 128 : side * 128 + 128, span] = dot(x, layer_v[span, :], NT).astype(BF16)
        own = dot(x, vw_four, NT)
        return jnp.where(quarter == lax.rem(group, 4), own, F32(0.0))

    own_home = project(0)
    pltpu.make_async_copy(weight_bytes(1), weight_bytes(1), w_recv.at[2]).wait()
    for q in (4, 2, 6):
        send_weight(q, flip(yh, 1), 1)
    x_pair.wait_recv()
    own_away = project(1)

    def partial(side, k, own):
        at = flip(tp_hi, k)
        weighted = cot_v[:, pl.ds(pl.multiple_of(at * 256, 256), 256)]
        a = a_v[side * 128 : side * 128 + 128, :]
        return jnp.where(own_chunk == at, own, F32(0.0)) - dot(a, weighted, NN) * inv_resp

    order = (3, 1, 2, 0)
    copies = {}
    for k in order:
        part = partial(1, k, own_away)
        for j in range(2):
            away_v[k, j] = part[:, j * 128 : (j + 1) * 128]
        copies[k] = pltpu.make_async_remote_copy(
            src_ref=away_v.at[k],
            dst_ref=core_v.at[k],
            send_sem=core_send.at[k],
            recv_sem=core_recv.at[k],
            device_id=device(0, 1, 0),
            device_id_type=MESH,
        )
        copies[k].start()
    pairs = [pass_on(0)]
    pl.semaphore_wait(ready_sem, 7)

    pairs.append(pass_on(1))
    for k in order:
        part = partial(0, k, own_home)
        copies[k].wait_recv()
        for j in range(2):
            home_v[k, j] = part[:, j * 128 : (j + 1) * 128] + core_v[k, j]
        for e in (0, 1) if k == 1 else (1, 0):
            j = flip(tp_lo, e)
            dt = 2 * k + e
            for q in (5, 3, 7, 4, 1, 2, 6, 0):
                if q or dt:
                    pltpu.make_async_remote_copy(
                        src_ref=home_v.at[k, j, pl.ds(q * 16, 16)],
                        dst_ref=recv_v.at[q * 8 + dt],
                        send_sem=rs_send,
                        recv_sem=rs_recv,
                        device_id=device(q, 0, dt),
                        device_id_type=MESH,
                    ).start()
    recv_v[0] = home_v[0, tp_lo, 0:16, :]

    for copy in pairs:
        copy.wait()
    wall = wall_v[...].reshape(wide, cols)
    held = grad_ref.shape[0]
    blk = held // 2
    for j in range(held // blk):
        span = slice(j * blk, (j + 1) * blk)
        grad_ref[span, :] = dot(cot_v[span, :], wall, NN).astype(BF16)

    pltpu.make_async_copy(recv_v.at[pl.ds(1, 63)], recv_v.at[pl.ds(1, 63)], rs_recv).wait()
    new_values = jnp.sum(recv_v[...], axis=0).astype(BF16)
    nv_ref[...] = new_values

    pltpu.make_async_copy(recv_v.at[pl.ds(1, 63)], recv_v.at[pl.ds(1, 63)], rs_send).wait()
    pltpu.make_async_copy(xall_v.at[pl.ds(1, 7)], xall_v.at[pl.ds(1, 7)], x_send).wait()
    x_pair.wait_send()
    for at, n in enumerate((3, 3, 1)):
        pltpu.make_async_copy(weight_bytes(n), weight_bytes(n), w_send.at[at]).wait()
    for k in range(4):
        copies[k].wait_send()


def finish(
    held_ref,
    nk_ref,
    nv_ref,
    att_ref,
    fresh_ref,
    perm_ref,
    cot_ref,
    wall_ref,
    grad_ref,
    nk_out,
    nv_out,
    att_out,
    zero_v,
    last_v,
    sem,
    zero_sem,
):
    done_n = held_ref.shape[0] // LIVE
    copies = []

    def write(src, at, rows, to):
        copy = pltpu.make_async_copy(src.at[pl.ds(at, rows)], grad_ref.at[pl.ds(to, rows)], sem.at[len(copies)])
        copy.start()
        copies.append(copy)

    for s in range(done_n):
        write(held_ref, s * LIVE, LIVE, s * SEQ_LEN + SKIP)
    zero_v[...] = jnp.zeros_like(zero_v)
    zeros = [
        pltpu.make_async_copy(zero_v, grad_ref.at[pl.ds(s * SEQ_LEN, SKIP)], zero_sem.at[s])
        for s in range(done_n + 1)
    ]
    for copy in zeros:
        copy.start()
    wide = cot_ref.shape[1]
    wall = wall_ref[...].reshape(wide, held_ref.shape[1])
    half = LIVE // 2
    for j in range(2):
        last_v[j * half : (j + 1) * half, :] = dot(
            cot_ref[done_n * LIVE + j * half : done_n * LIVE + (j + 1) * half, :], wall, NN
        ).astype(BF16)
        write(last_v, j * half, half, done_n * SEQ_LEN + SKIP + j * half)
    rows_n = nk_out.shape[1]
    done = (att_ref[...] + dot(fresh_ref[...], nv_ref[...], NN)).astype(BF16)
    back = dot(perm_ref[...], done, (((0,), (0,)), ((), ())))
    attended = jnp.concatenate([back[h * 16 : (h + 1) * 16] for h in range(QPK)], axis=1)
    for value, dst in (
        (nk_ref[...].astype(F32), nk_out),
        (nv_ref[...].astype(F32), nv_out),
        (attended, att_out),
    ):
        for s in range(dst.shape[0]):
            dst[s] = value[s * rows_n : (s + 1) * rows_n].astype(BF16)
    for copy in copies + zeros:
        copy.wait()


def body(*args):
    layer, cot, vw, rewards, groups, prompts, step, query, kw, ck, cv, lengths = args
    steps_n, rows_n, width = step.shape
    n = steps_n * rows_n
    seqs = layer.shape[0] // SEQ_LEN
    tokens = seqs * LIVE
    cols = layer.shape[1]
    hbm = pl.BlockSpec(memory_space=pl.ANY)
    smem = pl.BlockSpec(memory_space=pltpu.SMEM)
    vmem = pl.BlockSpec(memory_space=pltpu.VMEM)
    dma = pltpu.SemaphoreType.DMA
    results = pl.pallas_call(
        kernel,
        out_shape=(
            pltpu.VMEM((tokens - LIVE, cols), BF16),
            pltpu.VMEM((n, HEAD), BF16),
            pltpu.VMEM((n, HEAD), BF16),
            pltpu.VMEM((n * QPK, HEAD), F32),
            pltpu.VMEM((n * QPK, n), BF16),
            pltpu.VMEM((n * QPK, n * QPK), BF16),
            pltpu.VMEM((tokens, cot.shape[1]), BF16),
            pltpu.VMEM((4, 2, 2, *vw.shape), BF16),
        ),
        in_specs=[hbm, hbm, hbm, smem, smem, smem, hbm, hbm, hbm, hbm, hbm, smem],
        out_specs=(vmem,) * 8,
        scratch_shapes=[
            pltpu.VMEM((tokens, cols), BF16),
            pltpu.VMEM(vw.shape, BF16),
            pltpu.VMEM(step.shape, BF16),
            pltpu.VMEM(query.shape, BF16),
            pltpu.VMEM(kw.shape, BF16),
            pltpu.VMEM(ck.shape, BF16),
            pltpu.VMEM(cv.shape, BF16),
            pltpu.VMEM((n, width), BF16),
            pltpu.VMEM((16, n, cols), BF16),
            pltpu.VMEM((256, tokens), BF16),
            pltpu.VMEM((4, 2, 128, 128), F32),
            pltpu.VMEM((4, 2, 128, 128), F32),
            pltpu.VMEM((4, 2, 128, 128), F32),
            pltpu.VMEM((64, n, HEAD), F32),
            dma((20,)),
            dma,
            dma,
            dma,
            dma,
            dma((3,)),
            dma((3,)),
            dma((2,)),
            dma((2,)),
            dma((4,)),
            dma((4,)),
            dma,
            dma,
            pltpu.SemaphoreType.REGULAR,
        ],
        compiler_params=pltpu.CompilerParams(
            collective_id=0, has_side_effects=True, vmem_limit_bytes=46 * 1024 * 1024
        ),
    )(*(pltpu.with_memory_space_constraint(v, pltpu.HBM) if v.dtype == BF16 else v for v in args))
    held = [pltpu.with_memory_space_constraint(v, pltpu.VMEM) for v in results]
    return pl.pallas_call(
        finish,
        out_shape=(
            jax.ShapeDtypeStruct(layer.shape, BF16),
            jax.ShapeDtypeStruct((steps_n, rows_n, HEAD), BF16),
            jax.ShapeDtypeStruct((steps_n, rows_n, HEAD), BF16),
            jax.ShapeDtypeStruct((steps_n, rows_n, QPK * HEAD), BF16),
        ),
        in_specs=[vmem] * 8,
        out_specs=(hbm, vmem, vmem, vmem),
        scratch_shapes=[
            pltpu.VMEM((SKIP, cols), BF16),
            pltpu.VMEM((LIVE, cols), BF16),
            dma((seqs + 1,)),
            dma((seqs,)),
        ],
        compiler_params=pltpu.CompilerParams(vmem_limit_bytes=8 * 1024 * 1024),
    )(*held)


def solution(mesh):
    tokens = ("sec", "fsdp")
    in_specs = (
        P(tokens, "tp"),
        P(tokens, None),
        P(tokens, "tp"),
        P(),
        P(),
        P(),
        P(None, tokens, None),
        P(None, tokens, "tp"),
        P("tp", None),
        P(tokens, None, "tp"),
        P(tokens, None, "tp"),
        P(tokens),
    )
    out_specs = (
        P(tokens, "tp"),
        P(None, tokens, "tp"),
        P(None, tokens, "tp"),
        P(None, tokens, "tp"),
    )
    return jax.shard_map(body, mesh=mesh, in_specs=in_specs, out_specs=out_specs, check_vma=False)
```

```python
import functools

import jax
import jax.numpy as jnp
from jax import lax
from jax.experimental import pallas as pl
from jax.experimental.pallas import tpu as pltpu
from jax.sharding import PartitionSpec as P

HEAD = 128
QPK = 8
SEQ_LEN = 1024
GROUP = 8
SKIP = 128
LIVE = SEQ_LEN - SKIP
MESH = pl.DeviceIdType.MESH
F32 = jnp.float32
BF16 = jnp.bfloat16
NT = (((1,), (1,)), ((), ()))
NN = (((1,), (0,)), ((), ()))


def flip(value, bits):
    for at in range(3):
        unit = 1 << at
        if bits & unit:
            value = value + unit - 2 * unit * lax.rem(lax.div(value, unit), 2)
    return value


def dot(a, b, dims):
    return lax.dot_general(a, b, dims, preferred_element_type=F32)


def kernel(
    layer_ref,
    cot_ref,
    vw_ref,
    rewards_hbm,
    groups_hbm,
    prompts_hbm,
    step_ref,
    query_ref,
    kw_ref,
    ck_ref,
    cv_ref,
    len_hbm,
    grad_ref,
    nk_ref,
    nv_ref,
    att_ref,
    fresh_ref,
    perm_ref,
    cot_v,
    wall_v,
    rewards_ref,
    groups_ref,
    prompts_ref,
    len_ref,
    layer_v,
    vw_v,
    step_v,
    query_v,
    kw_v,
    ck_v,
    cv_v,
    flat_v,
    xall_v,
    a_v,
    away_v,
    home_v,
    core_v,
    recv_v,
    load_sem,
    x_send,
    x_recv,
    xp_send,
    xp_recv,
    w_send,
    w_recv,
    pair_send,
    pair_recv,
    core_send,
    core_recv,
    rs_send,
    rs_recv,
    ready_sem,
):
    sec = lax.axis_index("sec")
    fs = lax.axis_index("fsdp")
    tp = lax.axis_index("tp")
    core = lax.rem(fs, 2)
    yh = lax.div(fs, 2)
    group = sec * 4 + fs
    seqs = layer_ref.shape[0] // SEQ_LEN
    n_seq = rewards_hbm.shape[0]
    cols = layer_ref.shape[1]

    secs = [flip(sec, bits) for bits in range(4)]
    fss = [flip(fs, bits) for bits in range(4)]
    tps = [flip(tp, bits) for bits in range(8)]

    def device(q, dc, dt):
        return (secs[q // 2], fss[(q % 2) * 2 + dc], tps[dt])

    def near(q):
        return 4 * (q % 2)

    barrier = pltpu.get_barrier_semaphore()
    for q in (4, 5, 2, 3, 6, 7, 1):
        pl.semaphore_signal(barrier, inc=1, device_id=device(q, 0, near(q)), device_id_type=MESH)
    pl.semaphore_signal(barrier, inc=1, device_id=device(0, 1, 0), device_id_type=MESH)
    pl.semaphore_signal(barrier, inc=1, device_id=device(1, 0, 0), device_id_type=MESH)
    for dt in range(1, 8):
        pl.semaphore_signal(barrier, inc=1, device_id=device(0, 0, dt), device_id_type=MESH)

    def load(src, dst, at):
        copy = pltpu.make_async_copy(src, dst, load_sem.at[at])
        copy.start()
        return copy

    step_load = load(step_ref, step_v, 0)
    vw_load = load(vw_ref, vw_v, 1)
    scalar_loads = [
        load(src, dst, 20 + at)
        for at, (src, dst) in enumerate(
            (
                (rewards_hbm, rewards_ref),
                (groups_hbm, groups_ref),
                (prompts_hbm, prompts_ref),
                (len_hbm, len_ref),
            )
        )
    ]
    query_load = load(query_ref, query_v, 2)
    kw_load = load(kw_ref, kw_v, 3)
    rows_n = ck_ref.shape[0]
    ck_loads = [load(ck_ref.at[r], ck_v.at[r], 4 + r) for r in range(rows_n)]
    cv_loads = [load(cv_ref.at[r], cv_v.at[r], 8 + r) for r in range(rows_n)]
    cot_loads = [
        load(cot_ref.at[pl.ds(s * SEQ_LEN + SKIP, LIVE)], cot_v.at[pl.ds(s * LIVE, LIVE)], 12 + s)
        for s in range(seqs)
    ]
    layer_loads = [
        load(layer_ref.at[pl.ds(s * SEQ_LEN + SKIP, LIVE)], layer_v.at[pl.ds(s * LIVE, LIVE)], 16 + s)
        for s in range(seqs)
    ]

    step_load.wait()
    flat_v[...] = jnp.concatenate(
        [step_v[s].astype(F32) for s in range(step_v.shape[0])], axis=0
    ).astype(BF16)
    xall_v[0] = flat_v[:, pl.ds(pl.multiple_of(tp * cols, 128), cols)]
    vw_load.wait()
    wall_v[sec, yh, core] = vw_v[...]

    kw_load.wait()
    new_keys = dot(flat_v[...], kw_v[...], NT).astype(BF16)
    nk_ref[...] = new_keys

    pl.semaphore_wait(barrier, 16)
    for q in (4, 5, 2, 3, 6, 7, 1):
        at = pl.multiple_of(flip(tp, near(q)) * cols, 128)
        pltpu.make_async_remote_copy(
            src_ref=flat_v.at[:, pl.ds(at, cols)],
            dst_ref=xall_v.at[q],
            send_sem=x_send,
            recv_sem=x_recv,
            device_id=device(q, 0, near(q)),
            device_id_type=MESH,
        ).start()
    for dt in range(1, 8):
        pl.semaphore_signal(ready_sem, inc=1, device_id=device(0, 0, dt), device_id_type=MESH)

    def send_weight(q, half_at, at):
        pltpu.make_async_remote_copy(
            src_ref=wall_v.at[sec, half_at, core],
            dst_ref=wall_v.at[sec, half_at, core],
            send_sem=w_send.at[at],
            recv_sem=w_recv.at[at],
            device_id=device(q, 0, 0),
            device_id_type=MESH,
        ).start()

    def weight_bytes(n):
        return wall_v.at[pl.ds(0, n), 0, 0]

    send_weight(1, yh, 2)
    for q in (4, 2, 6):
        send_weight(q, yh, 0)

    for copy in scalar_loads:
        copy.wait()
    first = group * seqs
    own_groups = [groups_ref[first + s] for s in range(seqs)]
    own_prompts = [prompts_ref[first + s] for s in range(seqs)]

    def scan(j, carry):
        prompts = carry[0] + prompts_ref[j]
        reward = rewards_ref[j]
        sums = [
            c + jnp.where(groups_ref[j] == g, reward, F32(0.0))
            for c, g in zip(carry[1:], own_groups)
        ]
        return (prompts, *sums)

    scanned = lax.fori_loop(0, n_seq, scan, (jnp.int32(0),) + (F32(0.0),) * seqs)
    responses = (n_seq * SEQ_LEN - scanned[0]).astype(F32)
    advantage = [rewards_ref[first + s] - scanned[1 + s] / F32(GROUP) for s in range(seqs)]

    query_load.wait()
    steps_n = query_v.shape[0]
    q16 = jnp.concatenate([query_v[s].astype(F32) for s in range(steps_n)], axis=0).astype(BF16)
    stacked = jnp.concatenate([q16[:, h * HEAD : (h + 1) * HEAD] for h in range(QPK)], axis=0)
    n_q = QPK * steps_n * rows_n
    to_r = lax.broadcasted_iota(jnp.int32, (n_q, n_q), 0)
    frm = lax.broadcasted_iota(jnp.int32, (n_q, n_q), 1)
    per = steps_n * QPK
    src_of = lax.rem(to_r, QPK) * 16 + lax.rem(lax.div(to_r, QPK), steps_n) * rows_n + lax.div(to_r, per)
    perm = (frm == src_of).astype(F32).astype(BF16)
    scale = F32(1.0 / HEAD**0.5)
    queries = dot(perm, stacked, NN).astype(BF16)
    fresh = dot(queries, new_keys, NT) * scale
    i_at = lax.broadcasted_iota(jnp.int32, fresh.shape, 0)
    j_at = lax.broadcasted_iota(jnp.int32, fresh.shape, 1)
    causal = (lax.div(i_at, per) == lax.rem(j_at, rows_n)) & (
        lax.div(j_at, rows_n) <= lax.rem(lax.div(i_at, QPK), steps_n)
    )
    fresh = jnp.where(causal, fresh, F32(-1e30))
    fresh_top = jnp.max(fresh, axis=1, keepdims=True)
    slots = ck_v.shape[1]
    slot_at = lax.broadcasted_iota(jnp.int32, (per, slots), 1)
    for copy in ck_loads + cv_loads:
        copy.wait()
    parts = [slice(r * per, (r + 1) * per) for r in range(rows_n)]
    raw = [dot(queries[parts[r]], ck_v[r], NT) * scale for r in range(rows_n)]
    raw = [jnp.where(slot_at < len_ref[r], raw[r], F32(-1e30)) for r in range(rows_n)]
    tops = [jnp.maximum(jnp.max(raw[r], axis=1, keepdims=True), fresh_top[parts[r]]) for r in range(rows_n)]
    exps = [jnp.exp(raw[r] - tops[r]) for r in range(rows_n)]
    fresh_exps = [jnp.exp(fresh[parts[r]] - tops[r]) for r in range(rows_n)]
    fresh_probs = []
    for r in range(rows_n):
        total = jnp.sum(exps[r], axis=1, keepdims=True) + jnp.sum(fresh_exps[r], axis=1, keepdims=True)
        inv = F32(1.0) / total
        att_ref[parts[r], :] = dot((exps[r] * inv).astype(BF16), cv_v[r], NN)
        fresh_probs.append((fresh_exps[r] * inv).astype(BF16).astype(F32))
    fresh_ref[...] = jnp.concatenate(fresh_probs, axis=0).astype(BF16)
    perm_ref[...] = perm

    rows_at = lax.broadcasted_iota(jnp.int32, (128, 128), 0)
    wide = cot_v.shape[1]
    for s in range(seqs):
        cot_loads[s].wait()
        if s == seqs - 1:
            pltpu.make_async_copy(xall_v.at[pl.ds(1, 7)], xall_v.at[pl.ds(1, 7)], x_recv).wait()
            x_pair = pltpu.make_async_remote_copy(
                src_ref=xall_v.at[pl.ds(0, 8)],
                dst_ref=xall_v.at[pl.ds(8, 8)],
                send_sem=xp_send,
                recv_sem=xp_recv,
                device_id=device(0, 1, 0),
                device_id_type=MESH,
            )
            x_pair.start()

        def weigh(j, _, s=s):
            at = pl.multiple_of(s * LIVE + j * 128, 128)
            weight = jnp.where(rows_at + (SKIP + j * 128) >= own_prompts[s], advantage[s], F32(0.0))
            for n in range(wide // 128):
                span = slice(n * 128, (n + 1) * 128)
                cot_v[pl.ds(at, 128), span] = (cot_v[pl.ds(at, 128), span].astype(F32) * weight).astype(BF16)
            return 0

        lax.fori_loop(0, LIVE // 128, weigh, 0)

    def pass_on(batch):
        half_at = flip(yh, batch)
        pltpu.make_async_copy(weight_bytes(3), weight_bytes(3), w_recv.at[batch]).wait()
        copy = pltpu.make_async_remote_copy(
            src_ref=wall_v.at[:, half_at, core],
            dst_ref=wall_v.at[:, half_at, core],
            send_sem=pair_send.at[batch],
            recv_sem=pair_recv.at[batch],
            device_id=device(0, 1, 0),
            device_id_type=MESH,
        )
        copy.start()
        return copy

    inv_resp = F32(1.0) / responses
    quarter = lax.div(lax.broadcasted_iota(jnp.int32, (128, 256), 1), 64)
    own_chunk = lax.div(group, 4)
    tp_hi, tp_lo = lax.div(tp, 2), lax.rem(tp, 2)
    vw_four = jnp.concatenate([vw_v[...]] * 4, axis=0)

    def project(side):
        x = xall_v[side * 8 : side * 8 + 8].reshape(128, cols)
        for s in range(seqs):
            if not side:
                layer_loads[s].wait()
            span = slice(s * LIVE, (s + 1) * LIVE)
            a_v[side * 128 : side * 128 + 128, span] = dot(x, layer_v[span, :], NT).astype(BF16)
        own = dot(x, vw_four, NT)
        return jnp.where(quarter == lax.rem(group, 4), own, F32(0.0))

    own_home = project(0)
    pltpu.make_async_copy(weight_bytes(1), weight_bytes(1), w_recv.at[2]).wait()
    for q in (4, 2, 6):
        send_weight(q, flip(yh, 1), 1)
    x_pair.wait_recv()
    own_away = project(1)

    def partial(side, k, own):
        at = flip(tp_hi, k)
        weighted = cot_v[:, pl.ds(pl.multiple_of(at * 256, 256), 256)]
        a = a_v[side * 128 : side * 128 + 128, :]
        return jnp.where(own_chunk == at, own, F32(0.0)) - dot(a, weighted, NN) * inv_resp

    order = (3, 1, 2, 0)
    copies = {}
    for k in order:
        part = partial(1, k, own_away)
        for j in range(2):
            away_v[k, j] = part[:, j * 128 : (j + 1) * 128]
        copies[k] = pltpu.make_async_remote_copy(
            src_ref=away_v.at[k],
            dst_ref=core_v.at[k],
            send_sem=core_send.at[k],
            recv_sem=core_recv.at[k],
            device_id=device(0, 1, 0),
            device_id_type=MESH,
        )
        copies[k].start()
    pairs = [pass_on(0)]
    pl.semaphore_wait(ready_sem, 7)

    pairs.append(pass_on(1))
    for k in order:
        part = partial(0, k, own_home)
        copies[k].wait_recv()
        for j in range(2):
            home_v[k, j] = part[:, j * 128 : (j + 1) * 128] + core_v[k, j]
        for e in (0, 1) if k == 1 else (1, 0):
            j = flip(tp_lo, e)
            dt = 2 * k + e
            for q in (5, 3, 7, 4, 1, 2, 6, 0):
                if q or dt:
                    pltpu.make_async_remote_copy(
                        src_ref=home_v.at[k, j, pl.ds(q * 16, 16)],
                        dst_ref=recv_v.at[q * 8 + dt],
                        send_sem=rs_send,
                        recv_sem=rs_recv,
                        device_id=device(q, 0, dt),
                        device_id_type=MESH,
                    ).start()
    recv_v[0] = home_v[0, tp_lo, 0:16, :]

    for copy in pairs:
        copy.wait()
    wall = wall_v[...].reshape(wide, cols)
    held = grad_ref.shape[0]
    blk = held // 2
    for j in range(held // blk):
        span = slice(j * blk, (j + 1) * blk)
        grad_ref[span, :] = dot(cot_v[span, :], wall, NN).astype(BF16)

    pltpu.make_async_copy(recv_v.at[pl.ds(1, 63)], recv_v.at[pl.ds(1, 63)], rs_recv).wait()
    new_values = jnp.sum(recv_v[...], axis=0).astype(BF16)
    nv_ref[...] = new_values

    pltpu.make_async_copy(recv_v.at[pl.ds(1, 63)], recv_v.at[pl.ds(1, 63)], rs_send).wait()
    pltpu.make_async_copy(xall_v.at[pl.ds(1, 7)], xall_v.at[pl.ds(1, 7)], x_send).wait()
    x_pair.wait_send()
    for at, n in enumerate((3, 3, 1)):
        pltpu.make_async_copy(weight_bytes(n), weight_bytes(n), w_send.at[at]).wait()
    for k in range(4):
        copies[k].wait_send()


def finish(
    held_ref,
    nk_ref,
    nv_ref,
    att_ref,
    fresh_ref,
    perm_ref,
    cot_ref,
    wall_ref,
    grad_ref,
    nk_hbm,
    nv_hbm,
    att_hbm,
    nk_out,
    nv_out,
    att_out,
    zero_v,
    last_v,
    sem,
    zero_sem,
    small_sem,
):
    done_n = held_ref.shape[0] // LIVE
    copies = []

    def write(src, at, rows, to):
        copy = pltpu.make_async_copy(src.at[pl.ds(at, rows)], grad_ref.at[pl.ds(to, rows)], sem.at[len(copies)])
        copy.start()
        copies.append(copy)

    for s in range(done_n):
        write(held_ref, s * LIVE, LIVE, s * SEQ_LEN + SKIP)
    zero_v[...] = jnp.zeros_like(zero_v)
    zeros = [
        pltpu.make_async_copy(zero_v, grad_ref.at[pl.ds(s * SEQ_LEN, SKIP)], zero_sem.at[s])
        for s in range(done_n + 1)
    ]
    for copy in zeros:
        copy.start()
    rows_n = nk_out.shape[1]
    done = (att_ref[...] + dot(fresh_ref[...], nv_ref[...], NN)).astype(BF16)
    back = dot(perm_ref[...], done, (((0,), (0,)), ((), ())))
    attended = jnp.concatenate([back[h * 16 : (h + 1) * 16] for h in range(QPK)], axis=1)
    for value, dst in (
        (nk_ref[...].astype(F32), nk_out),
        (nv_ref[...].astype(F32), nv_out),
        (attended, att_out),
    ):
        for s in range(dst.shape[0]):
            dst[s] = value[s * rows_n : (s + 1) * rows_n].astype(BF16)
    small = [
        pltpu.make_async_copy(src, dst, small_sem.at[at])
        for at, (src, dst) in enumerate(((nk_out, nk_hbm), (nv_out, nv_hbm), (att_out, att_hbm)))
    ]
    for copy in small:
        copy.start()
    wide = cot_ref.shape[1]
    wall = wall_ref[...].reshape(wide, held_ref.shape[1])
    half = LIVE // 2
    for j in range(2):
        last_v[j * half : (j + 1) * half, :] = dot(
            cot_ref[done_n * LIVE + j * half : done_n * LIVE + (j + 1) * half, :], wall, NN
        ).astype(BF16)
        write(last_v, j * half, half, done_n * SEQ_LEN + SKIP + j * half)
    for copy in copies + zeros + small:
        copy.wait()


def body(*args):
    layer, cot, vw, rewards, groups, prompts, step, query, kw, ck, cv, lengths = args
    steps_n, rows_n, width = step.shape
    n = steps_n * rows_n
    seqs = layer.shape[0] // SEQ_LEN
    tokens = seqs * LIVE
    cols = layer.shape[1]
    hbm = pl.BlockSpec(memory_space=pl.ANY)
    vmem = pl.BlockSpec(memory_space=pltpu.VMEM)
    dma = pltpu.SemaphoreType.DMA
    results = pl.pallas_call(
        kernel,
        out_shape=(
            pltpu.VMEM((tokens - LIVE, cols), BF16),
            pltpu.VMEM((n, HEAD), BF16),
            pltpu.VMEM((n, HEAD), BF16),
            pltpu.VMEM((n * QPK, HEAD), F32),
            pltpu.VMEM((n * QPK, n), BF16),
            pltpu.VMEM((n * QPK, n * QPK), BF16),
            pltpu.VMEM((tokens, cot.shape[1]), BF16),
            pltpu.VMEM((4, 2, 2, *vw.shape), BF16),
        ),
        in_specs=[hbm] * 12,
        out_specs=(vmem,) * 8,
        scratch_shapes=[
            pltpu.SMEM(rewards.shape, F32),
            pltpu.SMEM(groups.shape, jnp.int32),
            pltpu.SMEM(prompts.shape, jnp.int32),
            pltpu.SMEM(lengths.shape, jnp.int32),
            pltpu.VMEM((tokens, cols), BF16),
            pltpu.VMEM(vw.shape, BF16),
            pltpu.VMEM(step.shape, BF16),
            pltpu.VMEM(query.shape, BF16),
            pltpu.VMEM(kw.shape, BF16),
            pltpu.VMEM(ck.shape, BF16),
            pltpu.VMEM(cv.shape, BF16),
            pltpu.VMEM((n, width), BF16),
            pltpu.VMEM((16, n, cols), BF16),
            pltpu.VMEM((256, tokens), BF16),
            pltpu.VMEM((4, 2, 128, 128), F32),
            pltpu.VMEM((4, 2, 128, 128), F32),
            pltpu.VMEM((4, 2, 128, 128), F32),
            pltpu.VMEM((64, n, HEAD), F32),
            dma((24,)),
            dma,
            dma,
            dma,
            dma,
            dma((3,)),
            dma((3,)),
            dma((2,)),
            dma((2,)),
            dma((4,)),
            dma((4,)),
            dma,
            dma,
            pltpu.SemaphoreType.REGULAR,
        ],
        compiler_params=pltpu.CompilerParams(
            collective_id=0, has_side_effects=True, vmem_limit_bytes=46 * 1024 * 1024
        ),
    )(*(pltpu.with_memory_space_constraint(v, pltpu.HBM) for v in args))
    held = [pltpu.with_memory_space_constraint(v, pltpu.VMEM) for v in results]
    return pl.pallas_call(
        finish,
        out_shape=(
            jax.ShapeDtypeStruct(layer.shape, BF16),
            jax.ShapeDtypeStruct((steps_n, rows_n, HEAD), BF16),
            jax.ShapeDtypeStruct((steps_n, rows_n, HEAD), BF16),
            jax.ShapeDtypeStruct((steps_n, rows_n, QPK * HEAD), BF16),
        ),
        in_specs=[vmem] * 8,
        out_specs=(hbm,) * 4,
        scratch_shapes=[
            pltpu.VMEM((steps_n, rows_n, HEAD), BF16),
            pltpu.VMEM((steps_n, rows_n, HEAD), BF16),
            pltpu.VMEM((steps_n, rows_n, QPK * HEAD), BF16),
            pltpu.VMEM((SKIP, cols), BF16),
            pltpu.VMEM((LIVE, cols), BF16),
            dma((seqs + 1,)),
            dma((seqs,)),
            dma((3,)),
        ],
        compiler_params=pltpu.CompilerParams(vmem_limit_bytes=8 * 1024 * 1024),
    )(*held)


def solution(mesh):
    tokens = ("sec", "fsdp")
    in_specs = (
        P(tokens, "tp"),
        P(tokens, None),
        P(tokens, "tp"),
        P(),
        P(),
        P(),
        P(None, tokens, None),
        P(None, tokens, "tp"),
        P("tp", None),
        P(tokens, None, "tp"),
        P(tokens, None, "tp"),
        P(tokens),
    )
    out_specs = (
        P(tokens, "tp"),
        P(None, tokens, "tp"),
        P(None, tokens, "tp"),
        P(None, tokens, "tp"),
    )
    return jax.shard_map(body, mesh=mesh, in_specs=in_specs, out_specs=out_specs, check_vma=False)
```

```python
import functools

import jax
import jax.numpy as jnp
from jax import lax
from jax.experimental import pallas as pl
from jax.experimental.pallas import tpu as pltpu
from jax.sharding import PartitionSpec as P

HEAD = 128
QPK = 8
SEQ_LEN = 1024
GROUP = 8
SKIP = 128
LIVE = SEQ_LEN - SKIP
MESH = pl.DeviceIdType.MESH
F32 = jnp.float32
BF16 = jnp.bfloat16
NT = (((1,), (1,)), ((), ()))
NN = (((1,), (0,)), ((), ()))


def flip(value, bits):
    for at in range(3):
        unit = 1 << at
        if bits & unit:
            value = value + unit - 2 * unit * lax.rem(lax.div(value, unit), 2)
    return value


def dot(a, b, dims):
    return lax.dot_general(a, b, dims, preferred_element_type=F32)


def kernel(
    layer_ref,
    cot_ref,
    vw_ref,
    rewards_hbm,
    groups_hbm,
    prompts_hbm,
    step_ref,
    query_ref,
    kw_ref,
    ck_ref,
    cv_ref,
    len_hbm,
    grad_ref,
    nk_ref,
    nv_ref,
    att_ref,
    fresh_ref,
    perm_ref,
    cot_v,
    wall_v,
    rewards_ref,
    groups_ref,
    prompts_ref,
    len_ref,
    layer_v,
    vw_v,
    step_v,
    query_v,
    kw_v,
    ck_v,
    cv_v,
    flat_v,
    xall_v,
    a_v,
    away_v,
    home_v,
    core_v,
    recv_v,
    load_sem,
    x_send,
    x_recv,
    xp_send,
    xp_recv,
    w_send,
    w_recv,
    pair_send,
    pair_recv,
    core_send,
    core_recv,
    rs_send,
    rs_recv,
    ready_sem,
):
    sec = lax.axis_index("sec")
    fs = lax.axis_index("fsdp")
    tp = lax.axis_index("tp")
    core = lax.rem(fs, 2)
    yh = lax.div(fs, 2)
    group = sec * 4 + fs
    seqs = layer_ref.shape[0] // SEQ_LEN
    n_seq = rewards_hbm.shape[0]
    cols = layer_ref.shape[1]

    secs = [flip(sec, bits) for bits in range(4)]
    fss = [flip(fs, bits) for bits in range(4)]
    tps = [flip(tp, bits) for bits in range(8)]

    def device(q, dc, dt):
        return (secs[q // 2], fss[(q % 2) * 2 + dc], tps[dt])

    def near(q):
        return 4 * (q % 2)

    barrier = pltpu.get_barrier_semaphore()
    for q in (4, 5, 2, 3, 6, 7, 1):
        pl.semaphore_signal(barrier, inc=1, device_id=device(q, 0, near(q)), device_id_type=MESH)
    pl.semaphore_signal(barrier, inc=1, device_id=device(0, 1, 0), device_id_type=MESH)
    pl.semaphore_signal(barrier, inc=1, device_id=device(1, 0, 0), device_id_type=MESH)
    for dt in range(1, 8):
        pl.semaphore_signal(barrier, inc=1, device_id=device(0, 0, dt), device_id_type=MESH)

    def load(src, dst, at):
        copy = pltpu.make_async_copy(src, dst, load_sem.at[at])
        copy.start()
        return copy

    step_load = load(step_ref, step_v, 0)
    vw_load = load(vw_ref, vw_v, 1)
    scalar_loads = [
        load(src, dst, 20 + at)
        for at, (src, dst) in enumerate(
            (
                (rewards_hbm, rewards_ref),
                (groups_hbm, groups_ref),
                (prompts_hbm, prompts_ref),
                (len_hbm, len_ref),
            )
        )
    ]
    query_load = load(query_ref, query_v, 2)
    kw_load = load(kw_ref, kw_v, 3)
    rows_n = ck_ref.shape[0]
    ck_loads = [load(ck_ref.at[r], ck_v.at[r], 4 + r) for r in range(rows_n)]
    cv_loads = [load(cv_ref.at[r], cv_v.at[r], 8 + r) for r in range(rows_n)]
    cot_loads = [
        load(cot_ref.at[pl.ds(s * SEQ_LEN + SKIP, LIVE)], cot_v.at[pl.ds(s * LIVE, LIVE)], 12 + s)
        for s in range(seqs)
    ]
    layer_loads = [
        load(layer_ref.at[pl.ds(s * SEQ_LEN + SKIP, LIVE)], layer_v.at[pl.ds(s * LIVE, LIVE)], 16 + s)
        for s in range(seqs)
    ]

    step_load.wait()
    flat_v[...] = jnp.concatenate(
        [step_v[s].astype(F32) for s in range(step_v.shape[0])], axis=0
    ).astype(BF16)
    xall_v[0] = flat_v[:, pl.ds(pl.multiple_of(tp * cols, 128), cols)]
    vw_load.wait()
    wall_v[sec, yh, core] = vw_v[...]

    kw_load.wait()
    new_keys = dot(flat_v[...], kw_v[...], NT).astype(BF16)
    nk_ref[...] = new_keys

    pl.semaphore_wait(barrier, 16)
    for q in (4, 5, 2, 3, 6, 7, 1):
        at = pl.multiple_of(flip(tp, near(q)) * cols, 128)
        pltpu.make_async_remote_copy(
            src_ref=flat_v.at[:, pl.ds(at, cols)],
            dst_ref=xall_v.at[q],
            send_sem=x_send,
            recv_sem=x_recv,
            device_id=device(q, 0, near(q)),
            device_id_type=MESH,
        ).start()
    for dt in range(1, 8):
        pl.semaphore_signal(ready_sem, inc=1, device_id=device(0, 0, dt), device_id_type=MESH)

    def send_weight(q, half_at, at):
        pltpu.make_async_remote_copy(
            src_ref=wall_v.at[sec, half_at, core],
            dst_ref=wall_v.at[sec, half_at, core],
            send_sem=w_send.at[at],
            recv_sem=w_recv.at[at],
            device_id=device(q, 0, 0),
            device_id_type=MESH,
        ).start()

    def weight_bytes(n):
        return wall_v.at[pl.ds(0, n), 0, 0]

    send_weight(1, yh, 2)
    for q in (4, 2, 6):
        send_weight(q, yh, 0)

    for copy in scalar_loads:
        copy.wait()
    first = group * seqs
    own_groups = [groups_ref[first + s] for s in range(seqs)]
    own_prompts = [prompts_ref[first + s] for s in range(seqs)]

    def scan(j, carry):
        prompts = carry[0] + prompts_ref[j]
        reward = rewards_ref[j]
        sums = [
            c + jnp.where(groups_ref[j] == g, reward, F32(0.0))
            for c, g in zip(carry[1:], own_groups)
        ]
        return (prompts, *sums)

    scanned = (jnp.int32(0),) + (F32(0.0),) * seqs
    for j in range(n_seq):
        scanned = scan(j, scanned)
    responses = (n_seq * SEQ_LEN - scanned[0]).astype(F32)
    advantage = [rewards_ref[first + s] - scanned[1 + s] / F32(GROUP) for s in range(seqs)]

    query_load.wait()
    steps_n = query_v.shape[0]
    q16 = jnp.concatenate([query_v[s].astype(F32) for s in range(steps_n)], axis=0).astype(BF16)
    stacked = jnp.concatenate([q16[:, h * HEAD : (h + 1) * HEAD] for h in range(QPK)], axis=0)
    n_q = QPK * steps_n * rows_n
    to_r = lax.broadcasted_iota(jnp.int32, (n_q, n_q), 0)
    frm = lax.broadcasted_iota(jnp.int32, (n_q, n_q), 1)
    per = steps_n * QPK
    src_of = lax.rem(to_r, QPK) * 16 + lax.rem(lax.div(to_r, QPK), steps_n) * rows_n + lax.div(to_r, per)
    perm = (frm == src_of).astype(F32).astype(BF16)
    scale = F32(1.0 / HEAD**0.5)
    queries = dot(perm, stacked, NN).astype(BF16)
    fresh = dot(queries, new_keys, NT) * scale
    i_at = lax.broadcasted_iota(jnp.int32, fresh.shape, 0)
    j_at = lax.broadcasted_iota(jnp.int32, fresh.shape, 1)
    causal = (lax.div(i_at, per) == lax.rem(j_at, rows_n)) & (
        lax.div(j_at, rows_n) <= lax.rem(lax.div(i_at, QPK), steps_n)
    )
    fresh = jnp.where(causal, fresh, F32(-1e30))
    fresh_top = jnp.max(fresh, axis=1, keepdims=True)
    slots = ck_v.shape[1]
    slot_at = lax.broadcasted_iota(jnp.int32, (per, slots), 1)
    for copy in ck_loads + cv_loads:
        copy.wait()
    parts = [slice(r * per, (r + 1) * per) for r in range(rows_n)]
    raw = [dot(queries[parts[r]], ck_v[r], NT) * scale for r in range(rows_n)]
    raw = [jnp.where(slot_at < len_ref[r], raw[r], F32(-1e30)) for r in range(rows_n)]
    tops = [jnp.maximum(jnp.max(raw[r], axis=1, keepdims=True), fresh_top[parts[r]]) for r in range(rows_n)]
    exps = [jnp.exp(raw[r] - tops[r]) for r in range(rows_n)]
    fresh_exps = [jnp.exp(fresh[parts[r]] - tops[r]) for r in range(rows_n)]
    fresh_probs = []
    for r in range(rows_n):
        total = jnp.sum(exps[r], axis=1, keepdims=True) + jnp.sum(fresh_exps[r], axis=1, keepdims=True)
        inv = F32(1.0) / total
        att_ref[parts[r], :] = dot((exps[r] * inv).astype(BF16), cv_v[r], NN)
        fresh_probs.append((fresh_exps[r] * inv).astype(BF16).astype(F32))
    fresh_ref[...] = jnp.concatenate(fresh_probs, axis=0).astype(BF16)
    perm_ref[...] = perm

    rows_at = lax.broadcasted_iota(jnp.int32, (128, 128), 0)
    wide = cot_v.shape[1]
    for s in range(seqs):
        cot_loads[s].wait()
        if s == seqs - 1:
            pltpu.make_async_copy(xall_v.at[pl.ds(1, 7)], xall_v.at[pl.ds(1, 7)], x_recv).wait()
            x_pair = pltpu.make_async_remote_copy(
                src_ref=xall_v.at[pl.ds(0, 8)],
                dst_ref=xall_v.at[pl.ds(8, 8)],
                send_sem=xp_send,
                recv_sem=xp_recv,
                device_id=device(0, 1, 0),
                device_id_type=MESH,
            )
            x_pair.start()

        def weigh(j, _, s=s):
            at = pl.multiple_of(s * LIVE + j * 128, 128)
            weight = jnp.where(rows_at + (SKIP + j * 128) >= own_prompts[s], advantage[s], F32(0.0))
            for n in range(wide // 128):
                span = slice(n * 128, (n + 1) * 128)
                cot_v[pl.ds(at, 128), span] = (cot_v[pl.ds(at, 128), span].astype(F32) * weight).astype(BF16)
            return 0

        lax.fori_loop(0, LIVE // 128, weigh, 0)

    def pass_on(batch):
        half_at = flip(yh, batch)
        pltpu.make_async_copy(weight_bytes(3), weight_bytes(3), w_recv.at[batch]).wait()
        copy = pltpu.make_async_remote_copy(
            src_ref=wall_v.at[:, half_at, core],
            dst_ref=wall_v.at[:, half_at, core],
            send_sem=pair_send.at[batch],
            recv_sem=pair_recv.at[batch],
            device_id=device(0, 1, 0),
            device_id_type=MESH,
        )
        copy.start()
        return copy

    inv_resp = F32(1.0) / responses
    quarter = lax.div(lax.broadcasted_iota(jnp.int32, (128, 256), 1), 64)
    own_chunk = lax.div(group, 4)
    tp_hi, tp_lo = lax.div(tp, 2), lax.rem(tp, 2)
    vw_four = jnp.concatenate([vw_v[...]] * 4, axis=0)

    def project(side):
        x = xall_v[side * 8 : side * 8 + 8].reshape(128, cols)
        for s in range(seqs):
            if not side:
                layer_loads[s].wait()
            span = slice(s * LIVE, (s + 1) * LIVE)
            a_v[side * 128 : side * 128 + 128, span] = dot(x, layer_v[span, :], NT).astype(BF16)
        own = dot(x, vw_four, NT)
        return jnp.where(quarter == lax.rem(group, 4), own, F32(0.0))

    own_home = project(0)
    pltpu.make_async_copy(weight_bytes(1), weight_bytes(1), w_recv.at[2]).wait()
    for q in (4, 2, 6):
        send_weight(q, flip(yh, 1), 1)
    x_pair.wait_recv()
    own_away = project(1)

    def partial(side, k, own):
        at = flip(tp_hi, k)
        weighted = cot_v[:, pl.ds(pl.multiple_of(at * 256, 256), 256)]
        a = a_v[side * 128 : side * 128 + 128, :]
        return jnp.where(own_chunk == at, own, F32(0.0)) - dot(a, weighted, NN) * inv_resp

    order = (3, 1, 2, 0)
    copies = {}
    for k in order:
        part = partial(1, k, own_away)
        for j in range(2):
            away_v[k, j] = part[:, j * 128 : (j + 1) * 128]
        copies[k] = pltpu.make_async_remote_copy(
            src_ref=away_v.at[k],
            dst_ref=core_v.at[k],
            send_sem=core_send.at[k],
            recv_sem=core_recv.at[k],
            device_id=device(0, 1, 0),
            device_id_type=MESH,
        )
        copies[k].start()
    pairs = [pass_on(0)]
    pl.semaphore_wait(ready_sem, 7)

    pairs.append(pass_on(1))
    for k in order:
        part = partial(0, k, own_home)
        copies[k].wait_recv()
        for j in range(2):
            home_v[k, j] = part[:, j * 128 : (j + 1) * 128] + core_v[k, j]
        for e in (0, 1) if k == 1 else (1, 0):
            j = flip(tp_lo, e)
            dt = 2 * k + e
            for q in (5, 3, 7, 4, 1, 2, 6, 0):
                if q or dt:
                    pltpu.make_async_remote_copy(
                        src_ref=home_v.at[k, j, pl.ds(q * 16, 16)],
                        dst_ref=recv_v.at[q * 8 + dt],
                        send_sem=rs_send,
                        recv_sem=rs_recv,
                        device_id=device(q, 0, dt),
                        device_id_type=MESH,
                    ).start()
    recv_v[0] = home_v[0, tp_lo, 0:16, :]

    for copy in pairs:
        copy.wait()
    wall = wall_v[...].reshape(wide, cols)
    held = grad_ref.shape[0]
    blk = held // 2
    for j in range(held // blk):
        span = slice(j * blk, (j + 1) * blk)
        grad_ref[span, :] = dot(cot_v[span, :], wall, NN).astype(BF16)

    pltpu.make_async_copy(recv_v.at[pl.ds(1, 63)], recv_v.at[pl.ds(1, 63)], rs_recv).wait()
    new_values = jnp.sum(recv_v[...], axis=0).astype(BF16)
    nv_ref[...] = new_values

    pltpu.make_async_copy(recv_v.at[pl.ds(1, 63)], recv_v.at[pl.ds(1, 63)], rs_send).wait()
    pltpu.make_async_copy(xall_v.at[pl.ds(1, 7)], xall_v.at[pl.ds(1, 7)], x_send).wait()
    x_pair.wait_send()
    for at, n in enumerate((3, 3, 1)):
        pltpu.make_async_copy(weight_bytes(n), weight_bytes(n), w_send.at[at]).wait()
    for k in range(4):
        copies[k].wait_send()


def finish(
    held_ref,
    nk_ref,
    nv_ref,
    att_ref,
    fresh_ref,
    perm_ref,
    cot_ref,
    wall_ref,
    grad_ref,
    nk_hbm,
    nv_hbm,
    att_hbm,
    nk_out,
    nv_out,
    att_out,
    zero_v,
    last_v,
    sem,
    zero_sem,
    small_sem,
):
    done_n = held_ref.shape[0] // LIVE
    copies = []

    def write(src, at, rows, to):
        copy = pltpu.make_async_copy(src.at[pl.ds(at, rows)], grad_ref.at[pl.ds(to, rows)], sem.at[len(copies)])
        copy.start()
        copies.append(copy)

    for s in range(done_n):
        write(held_ref, s * LIVE, LIVE, s * SEQ_LEN + SKIP)
    zero_v[...] = jnp.zeros_like(zero_v)
    zeros = [
        pltpu.make_async_copy(zero_v, grad_ref.at[pl.ds(s * SEQ_LEN, SKIP)], zero_sem.at[s])
        for s in range(done_n + 1)
    ]
    for copy in zeros:
        copy.start()
    rows_n = nk_out.shape[1]
    done = (att_ref[...] + dot(fresh_ref[...], nv_ref[...], NN)).astype(BF16)
    back = dot(perm_ref[...], done, (((0,), (0,)), ((), ())))
    attended = jnp.concatenate([back[h * 16 : (h + 1) * 16] for h in range(QPK)], axis=1)
    for value, dst in (
        (nk_ref[...].astype(F32), nk_out),
        (nv_ref[...].astype(F32), nv_out),
        (attended, att_out),
    ):
        for s in range(dst.shape[0]):
            dst[s] = value[s * rows_n : (s + 1) * rows_n].astype(BF16)
    small = [
        pltpu.make_async_copy(src, dst, small_sem.at[at])
        for at, (src, dst) in enumerate(((nk_out, nk_hbm), (nv_out, nv_hbm), (att_out, att_hbm)))
    ]
    for copy in small:
        copy.start()
    wide = cot_ref.shape[1]
    wall = wall_ref[...].reshape(wide, held_ref.shape[1])
    half = LIVE // 2
    for j in range(2):
        last_v[j * half : (j + 1) * half, :] = dot(
            cot_ref[done_n * LIVE + j * half : done_n * LIVE + (j + 1) * half, :], wall, NN
        ).astype(BF16)
        write(last_v, j * half, half, done_n * SEQ_LEN + SKIP + j * half)
    for copy in copies + zeros + small:
        copy.wait()


def body(*args):
    layer, cot, vw, rewards, groups, prompts, step, query, kw, ck, cv, lengths = args
    steps_n, rows_n, width = step.shape
    n = steps_n * rows_n
    seqs = layer.shape[0] // SEQ_LEN
    tokens = seqs * LIVE
    cols = layer.shape[1]
    hbm = pl.BlockSpec(memory_space=pl.ANY)
    vmem = pl.BlockSpec(memory_space=pltpu.VMEM)
    dma = pltpu.SemaphoreType.DMA
    results = pl.pallas_call(
        kernel,
        out_shape=(
            pltpu.VMEM((tokens - LIVE, cols), BF16),
            pltpu.VMEM((n, HEAD), BF16),
            pltpu.VMEM((n, HEAD), BF16),
            pltpu.VMEM((n * QPK, HEAD), F32),
            pltpu.VMEM((n * QPK, n), BF16),
            pltpu.VMEM((n * QPK, n * QPK), BF16),
            pltpu.VMEM((tokens, cot.shape[1]), BF16),
            pltpu.VMEM((4, 2, 2, *vw.shape), BF16),
        ),
        in_specs=[hbm] * 12,
        out_specs=(vmem,) * 8,
        scratch_shapes=[
            pltpu.SMEM(rewards.shape, F32),
            pltpu.SMEM(groups.shape, jnp.int32),
            pltpu.SMEM(prompts.shape, jnp.int32),
            pltpu.SMEM(lengths.shape, jnp.int32),
            pltpu.VMEM((tokens, cols), BF16),
            pltpu.VMEM(vw.shape, BF16),
            pltpu.VMEM(step.shape, BF16),
            pltpu.VMEM(query.shape, BF16),
            pltpu.VMEM(kw.shape, BF16),
            pltpu.VMEM(ck.shape, BF16),
            pltpu.VMEM(cv.shape, BF16),
            pltpu.VMEM((n, width), BF16),
            pltpu.VMEM((16, n, cols), BF16),
            pltpu.VMEM((256, tokens), BF16),
            pltpu.VMEM((4, 2, 128, 128), F32),
            pltpu.VMEM((4, 2, 128, 128), F32),
            pltpu.VMEM((4, 2, 128, 128), F32),
            pltpu.VMEM((64, n, HEAD), F32),
            dma((24,)),
            dma,
            dma,
            dma,
            dma,
            dma((3,)),
            dma((3,)),
            dma((2,)),
            dma((2,)),
            dma((4,)),
            dma((4,)),
            dma,
            dma,
            pltpu.SemaphoreType.REGULAR,
        ],
        compiler_params=pltpu.CompilerParams(
            collective_id=0, has_side_effects=True, vmem_limit_bytes=46 * 1024 * 1024
        ),
    )(*(pltpu.with_memory_space_constraint(v, pltpu.HBM) for v in args))
    held = [pltpu.with_memory_space_constraint(v, pltpu.VMEM) for v in results]
    return pl.pallas_call(
        finish,
        out_shape=(
            jax.ShapeDtypeStruct(layer.shape, BF16),
            jax.ShapeDtypeStruct((steps_n, rows_n, HEAD), BF16),
            jax.ShapeDtypeStruct((steps_n, rows_n, HEAD), BF16),
            jax.ShapeDtypeStruct((steps_n, rows_n, QPK * HEAD), BF16),
        ),
        in_specs=[vmem] * 8,
        out_specs=(hbm,) * 4,
        scratch_shapes=[
            pltpu.VMEM((steps_n, rows_n, HEAD), BF16),
            pltpu.VMEM((steps_n, rows_n, HEAD), BF16),
            pltpu.VMEM((steps_n, rows_n, QPK * HEAD), BF16),
            pltpu.VMEM((SKIP, cols), BF16),
            pltpu.VMEM((LIVE, cols), BF16),
            dma((seqs + 1,)),
            dma((seqs,)),
            dma((3,)),
        ],
        compiler_params=pltpu.CompilerParams(vmem_limit_bytes=8 * 1024 * 1024),
    )(*held)


def solution(mesh):
    tokens = ("sec", "fsdp")
    in_specs = (
        P(tokens, "tp"),
        P(tokens, None),
        P(tokens, "tp"),
        P(),
        P(),
        P(),
        P(None, tokens, None),
        P(None, tokens, "tp"),
        P("tp", None),
        P(tokens, None, "tp"),
        P(tokens, None, "tp"),
        P(tokens),
    )
    out_specs = (
        P(tokens, "tp"),
        P(None, tokens, "tp"),
        P(None, tokens, "tp"),
        P(None, tokens, "tp"),
    )
    return jax.shard_map(body, mesh=mesh, in_specs=in_specs, out_specs=out_specs, check_vma=False)
```
